1024 devices in a mesh: dp: 64 (over z, y_hi, core), bal: 4 (over x), tensor: 4 (over y_lo).
Axes of the slice: x: 4, y: 8 (y_hi: 2, y_lo: 4; y = y_hi * 4 + y_lo), z: 16, core: 2. Of those that a mesh axis runs over, the one named last changes fastest.
Arguments:
- tiles: bfloat16 [64, 4, 16, 1280, 128], P('dp', 'bal', None, 'tensor'), may hold values from -6 to 6
- tile_counts: int32 [64, 4], P('dp'), may hold values from 1 to 16, 32 in all within a row
- doc_order: int32 [64, 4], P('dp'), may hold values from 0 to 3, each once within a row
- qkv_weight: bfloat16 [3, 1280, 1280], P(None, 'dp', 'tensor'), may hold values from -6 to 6
- out_weight: bfloat16 [1280, 1280], P('dp', 'tensor'), may hold values from -0.625 to 0.625
Outputs:
- encoded: bfloat16 [64, 32, 1280, 128], P('dp', 'bal', 'tensor')
The draws below stay inside these ranges and needn't reach their ends.
Inputs may be any that keep to these rules, and one draw needn't show every extreme that they name: `tile_counts`: each row sums to 32, and in every row some document has exactly 16 tiles. `doc_order`: each row names every document once.
All inputs are finite; a program needn't handle non-finite values.
Results may differ from the reference program's by a relative error of at most 0.012.
Values may be sent and summed in bfloat16 or wider, within the bound.
No kernel may reach another device: no remote copies, remote signals or barrier semaphores. Data moves between devices by JAX's collectives and lax.ppermute only.
A program may use at most 64 MiB of HBM per device.

```python
import math
import jax
import jax.numpy as jnp
import numpy as np
from jax import lax

D = 1280
HEADS = 16
HDIM = 80
PATCH = 128
TILE_MAX = 16
CAP = 8
DOCS = 4
POSITIONS = 32
HEAD_GROUPS = 4
N_DP = 64


def draw_qkv_weight(key, part):
    standard = jnp.clip(jax.random.normal(key, (3, D, D), jnp.float32), -6.0, 6.0) * D ** (-0.5)
    return standard.astype(jnp.bfloat16)


def shard_levels(key, extent, pieces, smallest, high):
    def one(dim, shards_of):
        heights = jax.random.uniform(jax.random.fold_in(jax.random.fold_in(key, 6), dim), (shards_of,), jnp.float32, smallest / len(pieces), high / len(pieces))
        return jnp.repeat(jnp.exp(heights), extent[dim] // shards_of).reshape((-1,) + (1,) * (len(extent) - dim - 1))

    factor_of = one(*pieces[0])
    for cut in pieces[1:]:
        factor_of = factor_of * one(*cut)
    return factor_of


def length_profile(number_of, total, most, skew):
    portions = [(1 << 20) // math.isqrt(grade ** skew) + 1 for grade in range(2, number_of + 1)]
    surplus, given = total - most - (number_of - 1), [1] * (number_of - 1)
    while surplus > 0:
        candidates = [i for i in range(number_of - 1) if given[i] < most]
        mass, budget = sum([portions[i] for i in candidates]), surplus
        for i in candidates:
            more = min(most - given[i], max(1, budget * portions[i] // mass), surplus)
            given[i] = given[i] + more
            surplus = surplus - more
    return np.array([most] + given)


def ragged(own_key, amount, total, reach, skew):
    if amount == 2:
        one = jax.random.randint(own_key, (), max(1, total - reach), min(reach, total - 1) + 1)
        return jnp.stack([one, total - one])
    sizes = jnp.asarray(length_profile(amount, total, reach, skew), jnp.int32)
    couples = (amount - 1) // 2
    giver, sink = sizes[1:1 + 2 * couples:2], sizes[2:2 + 2 * couples:2]
    margin = jnp.minimum(giver - 1, reach - sink)
    shifted = jax.random.randint(jax.random.fold_in(own_key, 1), (couples,), 0, 1 << 20) % (margin + 1)
    sizes = sizes.at[1:1 + 2 * couples:2].set(giver - shifted).at[2:2 + 2 * couples:2].set(sink + shifted)
    return sizes[jax.random.permutation(jax.random.fold_in(own_key, 2), amount)]


def normal_values(rng, extent, deviation, most, split=(), kind=jnp.bfloat16):
    array = deviation * jax.random.normal(rng, extent, jnp.float32)
    if split:
        array = array * shard_levels(rng, extent, split, -0.22, 0.18)
    return jnp.clip(array, -most, most).astype(kind)


def setup_inputs(seed: int = 0) -> dict:
    key_list = jax.random.split(jax.random.key(seed), 6)
    tiles = normal_values(key_list[0], (N_DP, DOCS, TILE_MAX, D, PATCH), 1.0, 6.0, ((0, 64), (1, 4), (3, 4)))
    tile_counts = jax.vmap(lambda own: ragged(own, DOCS, POSITIONS, TILE_MAX, 2))(jax.random.split(key_list[1], N_DP)).reshape((N_DP, DOCS)).astype(jnp.int32)
    doc_order = jax.vmap(lambda own: jax.random.permutation(own, DOCS))(jax.random.split(key_list[2], N_DP)).reshape((N_DP, DOCS)).astype(jnp.int32)
    qkv_weight = draw_qkv_weight(jax.random.fold_in(key_list[5], 71), 0)
    out_weight = normal_values(key_list[4], (D, D), HDIM ** -0.5, 0.625, ((0, 64), (1, 4)))
    return {"tiles": tiles, "tile_counts": tile_counts, "doc_order": doc_order, "qkv_weight": qkv_weight, "out_weight": out_weight}


EPSILON = 1e-06

def normalize(tile_rows):
    values = tile_rows.astype(jnp.float32)
    center = values - lax.optimization_barrier(jnp.mean(values, axis=-1, keepdims=True))
    spread = lax.optimization_barrier(jnp.mean(center * center, axis=-1, keepdims=True))
    return (center * lax.rsqrt(spread + EPSILON)).astype(jnp.bfloat16)

def encode(tile_block, qkv_weight, out_weight):
    tile_total = tile_block.shape[0]
    row_count = tile_total * PATCH
    normed = normalize(tile_block).reshape(row_count, D)
    flat_weight = jnp.transpose(qkv_weight, (1, 0, 2)).reshape(D, 3 * D)
    projected = jnp.dot(normed, flat_weight, preferred_element_type=jnp.float32).astype(jnp.bfloat16)
    projected = projected.reshape(tile_total, PATCH, 3, HEADS, HDIM)
    query = projected[:, :, 0].astype(jnp.float32)
    key_rows = projected[:, :, 1].astype(jnp.float32)
    value_rows = projected[:, :, 2].astype(jnp.float32)
    scores = jnp.einsum('rqhe,rkhe->rhqk', query, key_rows) * HDIM ** (-0.5)
    probs = jax.nn.softmax(scores, axis=-1).astype(jnp.bfloat16)
    context = jnp.einsum('rhqk,rkhe->rqhe', probs.astype(jnp.float32), value_rows).astype(jnp.bfloat16)
    context = context.reshape(row_count, D)
    group_width = D // HEAD_GROUPS
    running = tile_block.astype(jnp.float32).reshape(row_count, D)
    for group in range(HEAD_GROUPS):
        low = group * group_width
        partial_value = jnp.dot(context[:, low:low + group_width], out_weight[:, low:low + group_width].T, preferred_element_type=jnp.float32)
        rounded = lax.optimization_barrier(partial_value.astype(jnp.bfloat16))
        running = running + rounded.astype(jnp.float32)
    return running.astype(jnp.bfloat16).reshape(tile_total, PATCH, D)

def reference(tiles, tile_counts, doc_order, qkv_weight, out_weight):
    doc_ids = jnp.arange(DOCS, dtype=jnp.int32)

    def group_index(counts, ordering):
        position = lax.optimization_barrier(jnp.sum(jnp.where(ordering[None, :] == doc_ids[:, None], doc_ids[None, :], 0), axis=1))
        starts = lax.optimization_barrier(jnp.sum(jnp.where(position[None, :] < position[:, None], counts[None, :], 0), axis=1))
        packed = jnp.arange(POSITIONS, dtype=jnp.int32)
        inside = (starts[None, :] <= packed[:, None]) & (packed[:, None] < (starts + counts)[None, :])
        source = lax.optimization_barrier(jnp.sum(jnp.where(inside, doc_ids[None, :], 0), axis=1))
        offset = packed - lax.optimization_barrier(jnp.sum(jnp.where(inside, starts[None, :], 0), axis=1))
        return (source * TILE_MAX + offset).astype(jnp.int32)
    flat_index = jax.vmap(group_index)(tile_counts, doc_order)
    group_base = (jnp.arange(N_DP, dtype=jnp.int32) * (DOCS * TILE_MAX)).astype(jnp.int32)
    flat_index = (flat_index + group_base[:, None]).astype(jnp.int32)
    flat_tiles = jnp.swapaxes(tiles, 3, 4).reshape(N_DP * DOCS * TILE_MAX, PATCH, D)
    packed_tiles = jnp.take(flat_tiles, flat_index.reshape(-1), axis=0)
    blocks = packed_tiles.reshape(N_DP * POSITIONS // CAP, CAP, PATCH, D)
    encoded = lax.map(lambda tile_block: encode(tile_block, qkv_weight, out_weight), blocks)
    return jnp.swapaxes(encoded.reshape(N_DP, POSITIONS, PATCH, D), 2, 3)
```

```python
import functools

import jax
import jax.numpy as jnp
from jax import lax
from jax.experimental import pallas as pl
from jax.experimental.pallas import tpu as pltpu
from jax.sharding import Mesh, PartitionSpec as P

D = 1280
HDIM = 80
PATCH = 128
SLOTS = 16
LOCAL = 2
WIDTH = LOCAL * HDIM
EPSILON = 1e-06
VMEM = 48 * 2**20


def vmem_params():
    return pltpu.CompilerParams(vmem_limit_bytes=VMEM)


def rotate_body(start_ref, tiles_ref, out_ref):
    start = start_ref[0]

    def one(slot, carry):
        out_ref[(slot + start) & (SLOTS - 1)] = tiles_ref[slot]
        return carry

    lax.fori_loop(0, SLOTS, one, 0)


def rotate(tiles, start):
    return pl.pallas_call(
        rotate_body,
        out_shape=jax.ShapeDtypeStruct(tiles.shape, tiles.dtype),
        in_specs=[pl.BlockSpec(memory_space=pltpu.SMEM), pl.BlockSpec(memory_space=pltpu.VMEM)],
        out_specs=pl.BlockSpec(memory_space=pltpu.VMEM),
        compiler_params=vmem_params(),
        name="rotate",
    )(start, tiles)


def normalise_body(pick_ref, tile_ref, source_ref, normed_ref):
    tile = tile_ref[0]
    source_ref[0] = tile
    values = tile.astype(jnp.float32)
    center = values - jnp.mean(values, axis=0, keepdims=True)
    spread = jnp.mean(center * center, axis=0, keepdims=True)
    normed_ref[0] = (center * lax.rsqrt(spread + EPSILON)).T.astype(jnp.bfloat16)


def normalise(arrived, pick):
    return pl.pallas_call(
        normalise_body,
        out_shape=(
            jax.ShapeDtypeStruct((2, D, PATCH), jnp.bfloat16),
            jax.ShapeDtypeStruct((2, PATCH, D), jnp.bfloat16),
        ),
        grid_spec=pltpu.PrefetchScalarGridSpec(
            num_scalar_prefetch=1,
            grid=(2,),
            in_specs=[pl.BlockSpec((1, D, PATCH), lambda j, pick: (pick[j], 0, 0))],
            out_specs=(
                pl.BlockSpec((1, D, PATCH), lambda j, pick: (j, 0, 0)),
                pl.BlockSpec((1, PATCH, D), lambda j, pick: (j, 0, 0)),
            ),
        ),
        compiler_params=vmem_params(),
        name="normalise",
    )(pick, arrived)


def attend(qkv):
    contexts = []
    for head in range(LOCAL):
        low = head * HDIM
        query = qkv[low : low + HDIM]
        key = qkv[WIDTH + low : WIDTH + low + HDIM]
        value = qkv[2 * WIDTH + low : 2 * WIDTH + low + HDIM]
        scores = lax.dot_general(
            key, query, (((0,), (0,)), ((), ())), preferred_element_type=jnp.float32
        ) * HDIM ** (-0.5)
        weights = jnp.exp(scores - jnp.max(scores, axis=0, keepdims=True))
        probs = (weights / jnp.sum(weights, axis=0, keepdims=True)).astype(jnp.bfloat16)
        contexts.append(jnp.dot(value, probs, preferred_element_type=jnp.float32))
    return jnp.concatenate(contexts, axis=0).astype(jnp.bfloat16)


def encode_body(own_ref, other_ref, weight_ref, own_out_ref, other_out_ref, total_ref):
    step = pl.program_id(0)
    weight = weight_ref[...].reshape(D, 4 * WIDTH)
    into = weight[:, : 3 * WIDTH]
    out = weight[:, 3 * WIDTH :]
    contexts = []
    for normed_ref in (own_ref, other_ref):
        normed = normed_ref[...].reshape(2 * PATCH, D)
        projected = jnp.dot(normed, into, preferred_element_type=jnp.float32)
        projected = projected.T.astype(jnp.bfloat16)
        for tile in range(2):
            contexts.append(attend(projected[:, tile * PATCH : (tile + 1) * PATCH]))
    context = jnp.concatenate(contexts, axis=1)
    partial_value = jnp.dot(out, context, preferred_element_type=jnp.float32)

    @pl.when(step == 0)
    def _():
        total_ref[...] = partial_value

    @pl.when(step > 0)
    def _():
        total_ref[...] += partial_value

    @pl.when(step == pl.num_programs(0) - 1)
    def _():
        for tile in range(4):
            target = (own_out_ref, other_out_ref)[tile // 2]
            block = total_ref[:, tile * PATCH : (tile + 1) * PATCH]
            target[tile % 2] = block.astype(jnp.bfloat16)


def encode(own, other, weights):
    steps = weights.shape[1]
    whole = pl.BlockSpec((2, PATCH, D), lambda s: (0, 0, 0))
    result = pl.BlockSpec((2, D, PATCH), lambda s: (0, 0, 0))
    part = jax.ShapeDtypeStruct((2, D, PATCH), jnp.bfloat16)
    return pl.pallas_call(
        encode_body,
        out_shape=(part, part),
        grid=(steps,),
        in_specs=[
            whole,
            whole,
            pl.BlockSpec(
                (weights.shape[0], 1, *weights.shape[2:]), lambda s: (0, s, 0, 0)
            ),
        ],
        out_specs=(result, result),
        scratch_shapes=[pltpu.VMEM((D, 4 * PATCH), jnp.float32)],
        compiler_params=vmem_params(),
        name="encode",
    )(own, other, weights)


def layout(counts, ordering):
    doc_ids = jnp.arange(counts.shape[0], dtype=jnp.int32)
    position = jnp.sum(
        jnp.where(ordering[None, :] == doc_ids[:, None], doc_ids[None, :], 0), axis=1
    )
    starts = jnp.sum(jnp.where(position[None, :] < position[:, None], counts[None, :], 0), axis=1)
    return doc_ids, starts


def local(tiles, tile_counts, doc_order, qkv_weight, out_weight):
    bal_hi, bal_lo = lax.axis_index("bal_hi"), lax.axis_index("bal_lo")
    tensor = lax.axis_index("tensor")
    swap = [(0, 1), (1, 0)]

    rows = qkv_weight.shape[1]
    kinds = [qkv_weight[k] for k in range(3)] + [out_weight]
    halves = jnp.stack(
        [
            jnp.concatenate([w[:, c * WIDTH : (c + 1) * WIDTH] for w in kinds], axis=1)
            for c in range(2)
        ]
    )
    outgoing = jnp.broadcast_to(halves[None, :, None], (2, 2, 4, rows, 4 * WIDTH))
    ring = lax.all_to_all(
        outgoing.reshape(16, rows, 4 * WIDTH), ("y_hi", "core", "tensor"), 0, 0, tiled=True
    )
    ring = ring.reshape(2, 2, 4, rows, 4 * WIDTH).transpose(2, 0, 1, 3, 4)
    ring = ring.reshape(4 * 4 * rows, 4 * WIDTH)
    weights = lax.all_gather(ring, "z", axis=0, tiled=True)
    weights = weights.reshape(-1, 4, 4 * rows, 4 * WIDTH)

    counts = tile_counts[0]
    doc_ids, starts = layout(counts, doc_order[0])
    ends = starts + counts
    own_start = jnp.sum(jnp.where(doc_ids == bal_hi * 2 + bal_lo, starts, 0))
    outbound = rotate(tiles[0, 0], own_start.reshape(1))
    outbound, ring = lax.optimization_barrier((outbound, ring))
    arrived = lax.all_to_all(outbound, ("bal_lo", "bal_hi", "tensor"), 0, 0, tiled=True)
    place = bal_lo * 8 + bal_hi * 4 + tensor
    packed = place + jnp.arange(2, dtype=jnp.int32) * SLOTS
    inside = (starts[None, :] <= packed[:, None]) & (packed[:, None] < ends[None, :])
    doc = jnp.sum(jnp.where(inside, doc_ids[None, :], 0), axis=1)
    source, normed = normalise(arrived.reshape(4, D, PATCH), doc % 2 * 2 + doc // 2)
    other = lax.ppermute(normed, "core", swap)

    own_part, other_part = encode(normed, other, weights)
    back_part = lax.ppermute(other_part, "core", swap)
    encoded = (
        source.astype(jnp.float32) + own_part.astype(jnp.float32) + back_part.astype(jnp.float32)
    ).astype(jnp.bfloat16)
    returned = lax.all_to_all(
        encoded.reshape(8, D // 4, PATCH), ("bal_hi", "tensor"), 0, 0, tiled=True
    )
    return returned[None]


def solution(mesh):
    z = mesh.shape["dp"] // 4
    devices = mesh.devices.reshape(z, 2, 2, 2, 2, 4)
    fine = Mesh(devices, ("z", "y_hi", "core", "bal_hi", "bal_lo", "tensor"))
    dp, bal = ("z", "y_hi", "core"), ("bal_hi", "bal_lo")
    placed = (
        P(dp, bal, None, "tensor", None),
        P(dp, None),
        P(dp, None),
        P(None, dp, "tensor"),
        P(dp, "tensor"),
    )
    return jax.shard_map(
        local, mesh=fine, in_specs=placed, out_specs=P(dp, bal, "tensor", None), check_vma=False
    )
```

```python
import functools

import jax
import jax.numpy as jnp
from jax import lax
from jax.experimental import pallas as pl
from jax.experimental.pallas import tpu as pltpu
from jax.sharding import Mesh, PartitionSpec as P

D = 1280
HDIM = 80
PATCH = 128
SLOTS = 16
BLOCKS = 16
LOCAL = 2
WIDTH = LOCAL * HDIM
EPSILON = 1e-06
VMEM = 24 * 2**20


def vmem_params():
    return pltpu.CompilerParams(vmem_limit_bytes=VMEM)


def rotate_body(start_ref, tiles_ref, out_ref):
    start = start_ref[0]

    def one(slot, carry):
        out_ref[(slot + start) & (SLOTS - 1)] = tiles_ref[slot]
        return carry

    lax.fori_loop(0, SLOTS, one, 0)


def rotate(tiles, start):
    return pl.pallas_call(
        rotate_body,
        out_shape=jax.ShapeDtypeStruct(tiles.shape, tiles.dtype),
        in_specs=[pl.BlockSpec(memory_space=pltpu.SMEM), pl.BlockSpec(memory_space=pltpu.VMEM)],
        out_specs=pl.BlockSpec(memory_space=pltpu.VMEM),
        compiler_params=vmem_params(),
        name="rotate",
    )(start, tiles)


def normalise_body(pick_ref, tile_ref, source_ref, normed_ref):
    tile = tile_ref[0]
    source_ref[0] = tile
    values = tile.astype(jnp.float32)
    center = values - jnp.mean(values, axis=0, keepdims=True)
    spread = jnp.mean(center * center, axis=0, keepdims=True)
    normed_ref[0] = (center * lax.rsqrt(spread + EPSILON)).T.astype(jnp.bfloat16)


def normalise(arrived, pick):
    return pl.pallas_call(
        normalise_body,
        out_shape=(
            jax.ShapeDtypeStruct((2, D, PATCH), jnp.bfloat16),
            jax.ShapeDtypeStruct((2, PATCH, D), jnp.bfloat16),
        ),
        grid_spec=pltpu.PrefetchScalarGridSpec(
            num_scalar_prefetch=1,
            grid=(2,),
            in_specs=[pl.BlockSpec((1, D, PATCH), lambda j, pick: (pick[j], 0, 0))],
            out_specs=(
                pl.BlockSpec((1, D, PATCH), lambda j, pick: (j, 0, 0)),
                pl.BlockSpec((1, PATCH, D), lambda j, pick: (j, 0, 0)),
            ),
        ),
        compiler_params=vmem_params(),
        name="normalise",
    )(pick, arrived)


def attend(qkv):
    contexts = []
    for head in range(LOCAL):
        low = head * HDIM
        query = qkv[low : low + HDIM]
        key = qkv[WIDTH + low : WIDTH + low + HDIM]
        value = qkv[2 * WIDTH + low : 2 * WIDTH + low + HDIM]
        scores = lax.dot_general(
            key, query, (((0,), (0,)), ((), ())), preferred_element_type=jnp.float32
        ) * HDIM ** (-0.5)
        weights = jnp.exp(scores - jnp.max(scores, axis=0, keepdims=True))
        probs = (weights / jnp.sum(weights, axis=0, keepdims=True)).astype(jnp.bfloat16)
        contexts.append(jnp.dot(value, probs, preferred_element_type=jnp.float32))
    return jnp.concatenate(contexts, axis=0).astype(jnp.bfloat16)


def block_z(where_ref, k):
    hop = (k + 1) // 2 * (1 if k % 2 else -1)
    return (where_ref[0] + where_ref[1] * hop) & (BLOCKS - 1)


def encode_body(where_ref, own_ref, other_ref, *refs):
    blocks = refs[:BLOCKS]
    own_out_ref, other_out_ref, weight_ref, total_ref, sems = refs[BLOCKS:]
    group_count = weight_ref.shape[1]

    def copies(group):
        return [
            pltpu.make_async_copy(
                block.at[group], weight_ref.at[block_z(where_ref, k), group], sems.at[group, k]
            )
            for k, block in enumerate(blocks)
        ]

    for group in range(group_count):
        for copy in copies(group):
            copy.start()
    for group in range(group_count):
        for copy in copies(group):
            copy.wait()
        weight = weight_ref[:, group].reshape(D, 4 * WIDTH)
        into = weight[:, : 3 * WIDTH]
        out = weight[:, 3 * WIDTH :]
        contexts = []
        for normed_ref in (own_ref, other_ref):
            normed = normed_ref[...].reshape(2 * PATCH, D)
            projected = jnp.dot(normed, into, preferred_element_type=jnp.float32)
            projected = projected.T.astype(jnp.bfloat16)
            for tile in range(2):
                contexts.append(attend(projected[:, tile * PATCH : (tile + 1) * PATCH]))
        context = jnp.concatenate(contexts, axis=1)
        partial_value = jnp.dot(out, context, preferred_element_type=jnp.float32)
        if group == 0:
            total_ref[...] = partial_value
        else:
            total_ref[...] += partial_value
    for tile in range(4):
        target = (own_out_ref, other_out_ref)[tile // 2]
        block = total_ref[:, tile * PATCH : (tile + 1) * PATCH]
        target[tile % 2] = block.astype(jnp.bfloat16)


def encode(where, own, other, blocks):
    in_vmem = pl.BlockSpec(memory_space=pltpu.VMEM)
    part = jax.ShapeDtypeStruct((2, D, PATCH), jnp.bfloat16)
    group_count = blocks[0].shape[0]
    return pl.pallas_call(
        encode_body,
        out_shape=(part, part),
        in_specs=[pl.BlockSpec(memory_space=pltpu.SMEM), in_vmem, in_vmem]
        + [pl.BlockSpec(memory_space=pl.ANY)] * len(blocks),
        out_specs=(in_vmem, in_vmem),
        scratch_shapes=[
            pltpu.VMEM((BLOCKS, *blocks[0].shape), jnp.bfloat16),
            pltpu.VMEM((D, 4 * PATCH), jnp.float32),
            pltpu.SemaphoreType.DMA((group_count, BLOCKS)),
        ],
        compiler_params=vmem_params(),
        name="encode",
    )(where, own, other, *[pltpu.with_memory_space_constraint(b, pltpu.HBM) for b in blocks])


def around_z(block):
    length = lax.axis_size("z")
    ways = (
        [(2 * i + c, (i + 1 - 2 * c) % length * 2 + c) for i in range(length) for c in range(2)],
        [(2 * i + c, (i - 1 + 2 * c) % length * 2 + c) for i in range(length) for c in range(2)],
    )
    held, blocks = [block, block], [block]
    for hop in range(1, length // 2 + 1):
        for chain in range(2 if 2 * hop < length else 1):
            held[chain] = lax.ppermute(held[chain], ("z", "core"), ways[chain])
            blocks.append(held[chain])
    return blocks


def layout(counts, ordering):
    doc_ids = jnp.arange(counts.shape[0], dtype=jnp.int32)
    position = jnp.sum(
        jnp.where(ordering[None, :] == doc_ids[:, None], doc_ids[None, :], 0), axis=1
    )
    starts = jnp.sum(jnp.where(position[None, :] < position[:, None], counts[None, :], 0), axis=1)
    return doc_ids, starts


def local(tiles, tile_counts, doc_order, qkv_weight, out_weight):
    bal_hi, bal_lo = lax.axis_index("bal_hi"), lax.axis_index("bal_lo")
    tensor = lax.axis_index("tensor")
    swap = [(0, 1), (1, 0)]

    rows = qkv_weight.shape[1]
    kinds = [qkv_weight[k] for k in range(3)] + [out_weight]
    halves = jnp.stack(
        [
            jnp.concatenate([w[:, c * WIDTH : (c + 1) * WIDTH] for w in kinds], axis=1)
            for c in range(2)
        ]
    )
    outgoing = jnp.broadcast_to(halves[None, :, None], (2, 2, 4, rows, 4 * WIDTH))
    ring = lax.all_to_all(
        outgoing.reshape(16, rows, 4 * WIDTH), ("y_hi", "core", "tensor"), 0, 0, tiled=True
    )
    block = ring.reshape(2, 2, 4, rows, 4 * WIDTH).transpose(2, 0, 1, 3, 4)
    blocks = around_z(block.reshape(4, 4 * rows, 4 * WIDTH))

    counts = tile_counts[0]
    doc_ids, starts = layout(counts, doc_order[0])
    ends = starts + counts
    own_start = jnp.sum(jnp.where(doc_ids == bal_hi * 2 + bal_lo, starts, 0))
    outbound = rotate(tiles[0, 0], own_start.reshape(1))
    outbound, ring = lax.optimization_barrier((outbound, ring))
    arrived = lax.all_to_all(outbound, ("bal_lo", "bal_hi", "tensor"), 0, 0, tiled=True)
    place = bal_lo * 8 + bal_hi * 4 + tensor
    packed = place + jnp.arange(2, dtype=jnp.int32) * SLOTS
    inside = (starts[None, :] <= packed[:, None]) & (packed[:, None] < ends[None, :])
    doc = jnp.sum(jnp.where(inside, doc_ids[None, :], 0), axis=1)
    source, normed = normalise(arrived.reshape(4, D, PATCH), doc % 2 * 2 + doc // 2)
    other = lax.ppermute(normed, "core", swap)

    where = jnp.stack([lax.axis_index("z"), 2 * lax.axis_index("core") - 1]).astype(jnp.int32)
    own_part, other_part = encode(where, normed, other, blocks)
    back_part = lax.ppermute(other_part, "core", swap)
    encoded = (
        source.astype(jnp.float32) + own_part.astype(jnp.float32) + back_part.astype(jnp.float32)
    ).astype(jnp.bfloat16)
    returned = lax.all_to_all(
        encoded.reshape(8, D // 4, PATCH), ("bal_hi", "tensor"), 0, 0, tiled=True
    )
    return returned[None]


def solution(mesh):
    z = mesh.shape["dp"] // 4
    devices = mesh.devices.reshape(z, 2, 2, 2, 2, 4)
    fine = Mesh(devices, ("z", "y_hi", "core", "bal_hi", "bal_lo", "tensor"))
    dp, bal = ("z", "y_hi", "core"), ("bal_hi", "bal_lo")
    placed = (
        P(dp, bal, None, "tensor", None),
        P(dp, None),
        P(dp, None),
        P(None, dp, "tensor"),
        P(dp, "tensor"),
    )
    return jax.shard_map(
        local, mesh=fine, in_specs=placed, out_specs=P(dp, bal, "tensor", None), check_vma=False
    )
```

```python
import jax
import jax.numpy as jnp
from jax import lax
from jax.experimental import pallas as pl
from jax.experimental.pallas import tpu as pltpu
from jax.sharding import Mesh, PartitionSpec as P

D = 1280
HDIM = 80
PATCH = 128
SLOTS = 16
ZS = 16
GROUPS = 4
PIECES = 4
LOCAL = 2
WIDTH = LOCAL * HDIM
EPSILON = 1e-06
VMEM = 32 * 2**20
LOG2E = 1.4426950408889634


def vmem_params():
    return pltpu.CompilerParams(vmem_limit_bytes=VMEM)


def rotate_body(start_ref, tiles_ref, out_ref):
    start = start_ref[0]

    def one(slot, carry):
        out_ref[(slot + start) & (SLOTS - 1)] = tiles_ref[slot]
        return carry

    lax.fori_loop(0, SLOTS, one, 0)


def rotate(tiles, start):
    return pl.pallas_call(
        rotate_body,
        out_shape=jax.ShapeDtypeStruct(tiles.shape, tiles.dtype),
        in_specs=[pl.BlockSpec(memory_space=pltpu.SMEM), pl.BlockSpec(memory_space=pltpu.VMEM)],
        out_specs=pl.BlockSpec(memory_space=pltpu.VMEM),
        compiler_params=vmem_params(),
        name="rotate",
    )(start, tiles)


def by_half(rows):
    parts = rows.reshape(ZS, 2, D // (2 * ZS), rows.shape[-1])
    return jnp.concatenate([parts[:, h].reshape(D // 2, rows.shape[-1]) for h in range(2)], axis=0)


def by_z(rows):
    parts = rows.reshape(2, ZS, 1, D // (2 * ZS), rows.shape[-1])
    return jnp.concatenate([parts[0], parts[1]], axis=1).reshape(D, rows.shape[-1])


def normalise_body(pick_ref, tile_ref, source_ref, normed_ref):
    tile = tile_ref[0]
    source_ref[0] = tile
    values = tile.astype(jnp.float32)
    center = values - jnp.mean(values, axis=0, keepdims=True)
    spread = jnp.mean(center * center, axis=0, keepdims=True)
    normed = by_half(center * lax.rsqrt(spread + EPSILON))
    normed_ref[0] = normed.T.astype(jnp.bfloat16)


def normalise(arrived, pick):
    return pl.pallas_call(
        normalise_body,
        out_shape=(
            jax.ShapeDtypeStruct((2, D, PATCH), jnp.bfloat16),
            jax.ShapeDtypeStruct((2, PATCH, D), jnp.bfloat16),
        ),
        grid_spec=pltpu.PrefetchScalarGridSpec(
            num_scalar_prefetch=1,
            grid=(2,),
            in_specs=[pl.BlockSpec((1, D, PATCH), lambda j, pick: (pick[j], 0, 0))],
            out_specs=(
                pl.BlockSpec((1, D, PATCH), lambda j, pick: (j, 0, 0)),
                pl.BlockSpec((1, PATCH, D), lambda j, pick: (j, 0, 0)),
            ),
        ),
        compiler_params=vmem_params(),
        name="normalise",
    )(pick, arrived)


def attend(qkv):
    pairs = [(tile, head) for tile in range(4) for head in range(LOCAL)]

    def part(kind, tile, head):
        low = kind * WIDTH + head * HDIM
        return qkv[low : low + HDIM, tile * PATCH : (tile + 1) * PATCH]

    scores = [
        lax.dot_general(
            part(1, *pair), part(0, *pair), (((0,), (0,)), ((), ())),
            preferred_element_type=jnp.float32,
        )
        for pair in pairs
    ]
    scale = HDIM ** (-0.5) * LOG2E
    powers = [jnp.exp2((s - jnp.max(s, axis=0, keepdims=True)) * scale) for s in scores]
    inverse = [1.0 / jnp.sum(p, axis=0, keepdims=True) for p in powers]
    contexts = [
        (
            jnp.dot(part(2, *pair), p.astype(jnp.bfloat16), preferred_element_type=jnp.float32) * i
        ).astype(jnp.bfloat16)
        for pair, p, i in zip(pairs, powers, inverse)
    ]
    return jnp.concatenate(
        [
            jnp.concatenate(contexts[tile * LOCAL : (tile + 1) * LOCAL], axis=0)
            for tile in range(4)
        ],
        axis=1,
    )


def encode_body(y_ref, own_ref, other_ref, *refs):
    pieces = refs[: GROUPS * PIECES]
    own_out_ref, other_out_ref, weight_ref, out_ref, context_ref, sems = refs[GROUPS * PIECES :]

    def copies(group):
        made = []
        for k in range(PIECES):
            y_hi = ((y_ref[0] + group + k // 2 * GROUPS) >> 2) & 1
            made.append(
                pltpu.make_async_copy(
                    pieces[group * PIECES + k], weight_ref.at[group, y_hi, k % 2], sems.at[group, k]
                )
            )
        return made

    for group in range(GROUPS):
        for copy in copies(group):
            copy.start()
    normed = jnp.concatenate(
        [ref[...].reshape(2 * PATCH, D) for ref in (own_ref, other_ref)], axis=0
    )
    for group in range(GROUPS):
        for copy in copies(group):
            copy.wait()
        weight = weight_ref[group].reshape(D, 4 * WIDTH)
        projected = jnp.dot(normed, weight[:, : 3 * WIDTH], preferred_element_type=jnp.float32)
        context_ref[group * WIDTH : (group + 1) * WIDTH] = attend(projected.astype(jnp.bfloat16).T)
        out_ref[group] = weight[:, 3 * WIDTH :]
    out = jnp.concatenate([out_ref[group] for group in range(GROUPS)], axis=1)
    total = by_z(jnp.dot(out, context_ref[...], preferred_element_type=jnp.float32))
    for tile in range(4):
        target = (own_out_ref, other_out_ref)[tile // 2]
        target[tile % 2] = total[:, tile * PATCH : (tile + 1) * PATCH].astype(jnp.bfloat16)


def encode(y, own, other, pieces):
    in_vmem = pl.BlockSpec(memory_space=pltpu.VMEM)
    part = jax.ShapeDtypeStruct((2, D, PATCH), jnp.bfloat16)
    in_hbm = [pltpu.with_memory_space_constraint(p, pltpu.HBM) for p in pieces]
    return pl.pallas_call(
        encode_body,
        out_shape=(part, part),
        in_specs=[pl.BlockSpec(memory_space=pltpu.SMEM), in_vmem, in_vmem]
        + [pl.BlockSpec(memory_space=pl.ANY)] * len(pieces),
        out_specs=(in_vmem, in_vmem),
        scratch_shapes=[
            pltpu.VMEM((GROUPS, 2, 2, D // 4, 4 * WIDTH), jnp.bfloat16),
            pltpu.VMEM((GROUPS, D, WIDTH), jnp.bfloat16),
            pltpu.VMEM((GROUPS * WIDTH, 4 * PATCH), jnp.bfloat16),
            pltpu.SemaphoreType.DMA((GROUPS, PIECES)),
        ],
        compiler_params=vmem_params(),
        name="encode",
    )(y, own, other, *in_hbm)


def around_y(block):
    length = 2 * GROUPS
    half = block.shape[0] // 2
    up = [(i, (i + 1) % length) for i in range(length)]
    down = [(i, (i - 1) % length) for i in range(length)]
    halves = [block[:half], block[half:]]
    rising, falling = list(halves), list(halves)
    found = {(0, 0): halves[0], (0, 1): halves[1]}
    for hop in range(1, length // 2 + 1):
        last = 2 * hop == length
        for k in range(2):
            if not last or k == 0:
                rising[k] = lax.ppermute(rising[k], ("y_hi", "tensor"), up)
                found[length - hop, k] = rising[k]
            if not last or k == 1:
                falling[k] = lax.ppermute(falling[k], ("y_hi", "tensor"), down)
                found[hop, k] = falling[k]
    return [
        found[group + k // 2 * GROUPS, k % 2] for group in range(GROUPS) for k in range(PIECES)
    ]


def layout(counts, ordering):
    doc_ids = jnp.arange(counts.shape[0], dtype=jnp.int32)
    position = jnp.sum(
        jnp.where(ordering[None, :] == doc_ids[:, None], doc_ids[None, :], 0), axis=1
    )
    starts = jnp.sum(jnp.where(position[None, :] < position[:, None], counts[None, :], 0), axis=1)
    return doc_ids, starts


def local(tiles, tile_counts, doc_order, qkv_weight, out_weight):
    bal_hi, bal_lo = lax.axis_index("bal_hi"), lax.axis_index("bal_lo")
    tensor = lax.axis_index("tensor")
    swap = [(0, 1), (1, 0)]

    rows = qkv_weight.shape[1]
    kinds = [qkv_weight[k] for k in range(3)] + [out_weight]
    halves = jnp.stack(
        [
            jnp.concatenate([w[:, c * WIDTH : (c + 1) * WIDTH] for w in kinds], axis=1)
            for c in range(2)
        ]
    )
    both = lax.all_to_all(halves, "core", 0, 0, tiled=True).reshape(2 * rows, 4 * WIDTH)

    counts = tile_counts[0]
    doc_ids, starts = layout(counts, doc_order[0])
    ends = starts + counts
    own_start = jnp.sum(jnp.where(doc_ids == bal_hi * 2 + bal_lo, starts, 0))
    outbound = rotate(tiles[0, 0], own_start.reshape(1))
    outbound, both = lax.optimization_barrier((outbound, both))
    arrived = lax.all_to_all(outbound, ("bal_lo", "bal_hi", "tensor"), 0, 0, tiled=True)
    block = lax.all_gather(both, "z", axis=0, tiled=True)
    pieces = around_y(block)
    place = bal_lo * 8 + bal_hi * 4 + tensor
    packed = place + jnp.arange(2, dtype=jnp.int32) * SLOTS
    inside = (starts[None, :] <= packed[:, None]) & (packed[:, None] < ends[None, :])
    doc = jnp.sum(jnp.where(inside, doc_ids[None, :], 0), axis=1)
    source, normed = normalise(arrived.reshape(4, D, PATCH), doc % 2 * 2 + doc // 2)
    other = lax.ppermute(normed, "core", swap)

    y = lax.axis_index("y_hi") * 4 + tensor
    own_part, other_part = encode(y.reshape(1).astype(jnp.int32), normed, other, pieces)
    back_part = lax.ppermute(other_part, "core", swap)
    encoded = (
        source.astype(jnp.float32) + own_part.astype(jnp.float32) + back_part.astype(jnp.float32)
    ).astype(jnp.bfloat16)
    returned = lax.all_to_all(
        encoded.reshape(8, D // 4, PATCH), ("bal_hi", "tensor"), 0, 0, tiled=True
    )
    return returned[None]


def solution(mesh):
    z = mesh.shape["dp"] // 4
    devices = mesh.devices.reshape(z, 2, 2, 2, 2, 4)
    fine = Mesh(devices, ("z", "y_hi", "core", "bal_hi", "bal_lo", "tensor"))
    dp, bal = ("z", "y_hi", "core"), ("bal_hi", "bal_lo")
    placed = (
        P(dp, bal, None, "tensor", None),
        P(dp, None),
        P(dp, None),
        P(None, dp, "tensor"),
        P(dp, "tensor"),
    )
    return jax.shard_map(
        local, mesh=fine, in_specs=placed, out_specs=P(dp, bal, "tensor", None), check_vma=False
    )
```

```python
import jax
import jax.numpy as jnp
from jax import lax
from jax.experimental import pallas as pl
from jax.experimental.pallas import tpu as pltpu
from jax.sharding import Mesh, PartitionSpec as P

D = 1280
HDIM = 80
PATCH = 128
SLOTS = 16
DOCS = 4
ZS = 16
GROUPS = 4
PIECES = 4
EARLY, LATE = (2, 1, 3), (0,)
LOCAL = 2
WIDTH = LOCAL * HDIM
EPSILON = 1e-06
VMEM = 32 * 2**20
LOG2E = 1.4426950408889634


def vmem_params():
    return pltpu.CompilerParams(vmem_limit_bytes=VMEM)


def cut_body(qkv_ref, out_ref, halves_ref):
    for core in range(2):
        low = core * WIDTH
        kinds = [qkv_ref[k, :, low : low + WIDTH] for k in range(3)] + [out_ref[:, low : low + WIDTH]]
        halves_ref[core] = jnp.concatenate(kinds, axis=1)


def cut(qkv_weight, out_weight):
    return pl.pallas_call(
        cut_body,
        out_shape=jax.ShapeDtypeStruct((2, out_weight.shape[0], 4 * WIDTH), jnp.bfloat16),
        compiler_params=vmem_params(),
        name="cut",
    )(qkv_weight, out_weight)


def in_turn(counts_ref, order_ref):
    first, turns = 0, []
    for turn in range(DOCS):
        doc = order_ref[turn]
        turns.append((doc, first, counts_ref[doc]))
        first = first + counts_ref[doc]
    return turns


def rotate_body(where_ref, counts_ref, order_ref, tiles_ref, out_ref, sems):
    start = 0
    for doc, first, _ in in_turn(counts_ref, order_ref):
        start = jnp.where(doc == where_ref[0], first, start)
    copies = [
        pltpu.make_async_copy(
            tiles_ref.at[slot], out_ref.at[(slot + start) & (SLOTS - 1)], sems.at[slot]
        )
        for slot in range(SLOTS)
    ]
    for copy in copies:
        copy.start()
    for copy in copies:
        copy.wait()


def rotate(where, counts, order, tiles):
    in_smem = pl.BlockSpec(memory_space=pltpu.SMEM)
    return pl.pallas_call(
        rotate_body,
        out_shape=jax.ShapeDtypeStruct(tiles.shape, tiles.dtype),
        in_specs=[in_smem, in_smem, in_smem, pl.BlockSpec(memory_space=pl.ANY)],
        out_specs=pl.BlockSpec(memory_space=pl.ANY),
        scratch_shapes=[pltpu.SemaphoreType.DMA((SLOTS,))],
        compiler_params=vmem_params(),
        name="rotate",
    )(where, counts, order, pltpu.with_memory_space_constraint(tiles, pltpu.HBM))


def by_half(rows):
    parts = rows.reshape(ZS, 2, D // (2 * ZS), rows.shape[-1])
    return jnp.concatenate([parts[:, h].reshape(D // 2, rows.shape[-1]) for h in range(2)], axis=0)


def by_z(rows):
    parts = rows.reshape(2, ZS, 1, D // (2 * ZS), rows.shape[-1])
    return jnp.concatenate([parts[0], parts[1]], axis=1).reshape(D, rows.shape[-1])


def normalise_body(where_ref, counts_ref, order_ref, tile_ref, source_ref, normed_ref):
    tile = tile_ref[0]
    source_ref[0] = tile
    values = tile.astype(jnp.float32)
    center = values - jnp.mean(values, axis=0, keepdims=True)
    spread = jnp.mean(center * center, axis=0, keepdims=True)
    normed = by_half(center * lax.rsqrt(spread + EPSILON))
    normed_ref[0] = normed.T.astype(jnp.bfloat16)


def normalise(where, counts, order, arrived):
    def pick(j, where_ref, counts_ref, order_ref):
        packed = where_ref[1] + j * SLOTS
        owner = 0
        for doc, first, count in in_turn(counts_ref, order_ref):
            owner = jnp.where((first <= packed) & (packed < first + count), doc, owner)
        return (owner & 1) * 2 + (owner >> 1), 0, 0

    def same(j, *_):
        return j, 0, 0

    return pl.pallas_call(
        normalise_body,
        out_shape=(
            jax.ShapeDtypeStruct((2, D, PATCH), jnp.bfloat16),
            jax.ShapeDtypeStruct((2, PATCH, D), jnp.bfloat16),
        ),
        grid_spec=pltpu.PrefetchScalarGridSpec(
            num_scalar_prefetch=3,
            grid=(2,),
            in_specs=[pl.BlockSpec((1, D, PATCH), pick)],
            out_specs=(pl.BlockSpec((1, D, PATCH), same), pl.BlockSpec((1, PATCH, D), same)),
        ),
        compiler_params=vmem_params(),
        name="normalise",
    )(where, counts, order, arrived)


def attend(qkv):
    pairs = [(tile, head) for tile in range(4) for head in range(LOCAL)]

    def part(kind, tile, head):
        low = kind * WIDTH + head * HDIM
        return qkv[low : low + HDIM, tile * PATCH : (tile + 1) * PATCH]

    scores = [
        lax.dot_general(
            part(1, *pair), part(0, *pair), (((0,), (0,)), ((), ())),
            preferred_element_type=jnp.float32,
        )
        for pair in pairs
    ]
    scale = HDIM ** (-0.5) * LOG2E
    powers = [jnp.exp2((s - jnp.max(s, axis=0, keepdims=True)) * scale) for s in scores]
    inverse = [1.0 / jnp.sum(p, axis=0, keepdims=True) for p in powers]
    contexts = [
        (
            jnp.dot(part(2, *pair), p.astype(jnp.bfloat16), preferred_element_type=jnp.float32) * i
        ).astype(jnp.bfloat16)
        for pair, p, i in zip(pairs, powers, inverse)
    ]
    return jnp.concatenate(
        [
            jnp.concatenate(contexts[tile * LOCAL : (tile + 1) * LOCAL], axis=0)
            for tile in range(4)
        ],
        axis=1,
    )


def group_contexts(groups, where_ref, own_ref, other_ref, pieces, weight_ref, sems):
    def copies(n, group):
        made = []
        for k in range(PIECES):
            y_hi = ((where_ref[2] + group + k // 2 * GROUPS) >> 2) & 1
            made.append(
                pltpu.make_async_copy(
                    pieces[n * PIECES + k], weight_ref.at[n, y_hi, k % 2], sems.at[n, k]
                )
            )
        return made

    for n, group in enumerate(groups):
        for copy in copies(n, group):
            copy.start()
    normed = jnp.concatenate(
        [ref[...].reshape(2 * PATCH, D) for ref in (own_ref, other_ref)], axis=0
    )
    contexts, outs = [], []
    for n, group in enumerate(groups):
        for copy in copies(n, group):
            copy.wait()
        weight = weight_ref[n].reshape(D, 4 * WIDTH)
        projected = jnp.dot(normed, weight[:, : 3 * WIDTH], preferred_element_type=jnp.float32)
        contexts.append(attend(projected.astype(jnp.bfloat16).T))
        outs.append(weight[:, 3 * WIDTH :])
    return jnp.dot(
        jnp.concatenate(outs, axis=1),
        jnp.concatenate(contexts, axis=0),
        preferred_element_type=jnp.float32,
    )


def early_body(where_ref, own_ref, other_ref, *refs):
    count = len(EARLY) * PIECES
    total_ref, weight_ref, sems = refs[count:]
    total_ref[...] = group_contexts(
        EARLY, where_ref, own_ref, other_ref, refs[:count], weight_ref, sems
    )


def late_body(where_ref, own_ref, other_ref, early_ref, *refs):
    count = len(LATE) * PIECES
    own_out_ref, other_out_ref, weight_ref, sems = refs[count:]
    total = group_contexts(LATE, where_ref, own_ref, other_ref, refs[:count], weight_ref, sems)
    total = by_z(total + early_ref[...])
    for tile in range(4):
        target = (own_out_ref, other_out_ref)[tile // 2]
        target[tile % 2] = total[:, tile * PATCH : (tile + 1) * PATCH].astype(jnp.bfloat16)


def encode(body, groups, out_shape, where, arrays, pieces):
    in_vmem = pl.BlockSpec(memory_space=pltpu.VMEM)
    taken = [pieces[group * PIECES + k] for group in groups for k in range(PIECES)]
    if groups == EARLY:
        taken = [pltpu.with_memory_space_constraint(t, pltpu.HBM) for t in taken]
    flops = 2 * 4 * PATCH * D * 4 * WIDTH * len(groups)
    return pl.pallas_call(
        body,
        out_shape=out_shape,
        in_specs=[pl.BlockSpec(memory_space=pltpu.SMEM)]
        + [in_vmem] * len(arrays)
        + [pl.BlockSpec(memory_space=pl.ANY)] * len(taken),
        out_specs=jax.tree.map(lambda _: in_vmem, out_shape),
        scratch_shapes=[
            pltpu.VMEM((len(groups), 2, 2, D // 4, 4 * WIDTH), jnp.bfloat16),
            pltpu.SemaphoreType.DMA((len(groups), PIECES)),
        ],
        compiler_params=vmem_params(),
        cost_estimate=pl.CostEstimate(
            flops=flops, bytes_accessed=len(groups) * D * 8 * WIDTH, transcendentals=0
        ),
        name=body.__name__,
    )(where, *arrays, *taken)


def around_y(block):
    length = 2 * GROUPS
    half = block.shape[0] // 2
    up = [(i, (i + 1) % length) for i in range(length)]
    down = [(i, (i - 1) % length) for i in range(length)]
    halves = [block[:half], block[half:]]
    rising, falling = list(halves), list(halves)
    found = {(0, 0): halves[0], (0, 1): halves[1]}
    for hop in range(1, length // 2 + 1):
        last = 2 * hop == length
        for k in range(2):
            if not last or k == 0:
                rising[k] = lax.ppermute(rising[k], ("y_hi", "tensor"), up)
                found[length - hop, k] = rising[k]
            if not last or k == 1:
                falling[k] = lax.ppermute(falling[k], ("y_hi", "tensor"), down)
                found[hop, k] = falling[k]
    return [
        found[group + k // 2 * GROUPS, k % 2] for group in range(GROUPS) for k in range(PIECES)
    ]


def local(tiles, tile_counts, doc_order, qkv_weight, out_weight):
    bal_hi, bal_lo = lax.axis_index("bal_hi"), lax.axis_index("bal_lo")
    tensor = lax.axis_index("tensor")
    swap = [(0, 1), (1, 0)]

    place = bal_lo * 8 + bal_hi * 4 + tensor
    y = lax.axis_index("y_hi") * 4 + tensor
    where = jnp.stack([bal_hi * 2 + bal_lo, place, y]).astype(jnp.int32)
    counts, order = tile_counts[0], doc_order[0]

    halves = cut(qkv_weight, out_weight)
    both = lax.all_to_all(halves, "core", 0, 0, tiled=True).reshape(-1, 4 * WIDTH)

    outbound = rotate(where, counts, order, tiles[0, 0])
    outbound, both = lax.optimization_barrier((outbound, both))
    arrived = lax.all_to_all(outbound, ("bal_lo", "bal_hi", "tensor"), 0, 0, tiled=True)
    block = lax.all_gather(both, "z", axis=0, tiled=True)
    pieces = around_y(block)
    source, normed = normalise(where, counts, order, arrived.reshape(4, D, PATCH))
    other = lax.ppermute(normed, "core", swap)

    early = jax.ShapeDtypeStruct((D, 4 * PATCH), jnp.float32)
    part = jax.ShapeDtypeStruct((2, D, PATCH), jnp.bfloat16)
    total = encode(early_body, EARLY, early, where, (normed, other), pieces)
    own_part, other_part = encode(
        late_body, LATE, (part, part), where, (normed, other, total), pieces
    )
    back_part = lax.ppermute(other_part, "core", swap)
    encoded = (
        source.astype(jnp.float32) + own_part.astype(jnp.float32) + back_part.astype(jnp.float32)
    ).astype(jnp.bfloat16)
    returned = lax.all_to_all(
        encoded.reshape(8, D // 4, PATCH), ("bal_hi", "tensor"), 0, 0, tiled=True
    )
    return returned[None]


def solution(mesh):
    z = mesh.shape["dp"] // 4
    devices = mesh.devices.reshape(z, 2, 2, 2, 2, 4)
    fine = Mesh(devices, ("z", "y_hi", "core", "bal_hi", "bal_lo", "tensor"))
    dp, bal = ("z", "y_hi", "core"), ("bal_hi", "bal_lo")
    placed = (
        P(dp, bal, None, "tensor", None),
        P(dp, None),
        P(dp, None),
        P(None, dp, "tensor"),
        P(dp, "tensor"),
    )
    return jax.shard_map(
        local, mesh=fine, in_specs=placed, out_specs=P(dp, bal, "tensor", None), check_vma=False
    )
```

```python
import jax
import jax.numpy as jnp
from jax import lax
from jax.experimental import pallas as pl
from jax.experimental.pallas import tpu as pltpu
from jax.sharding import Mesh, PartitionSpec as P

D = 1280
HDIM = 80
PATCH = 128
SLOTS = 16
DOCS = 4
ZS = 16
GROUPS = 4
PIECES = 4
EARLY, LATE = (2, 1, 3), (0,)
LOCAL = 2
WIDTH = LOCAL * HDIM
EPSILON = 1e-06
VMEM = 32 * 2**20
LOG2E = 1.4426950408889634


def vmem_params():
    return pltpu.CompilerParams(vmem_limit_bytes=VMEM)


def cut_body(qkv_ref, out_ref, halves_ref):
    for core in range(2):
        low = core * WIDTH
        kinds = [qkv_ref[k, :, low : low + WIDTH] for k in range(3)] + [out_ref[:, low : low + WIDTH]]
        halves_ref[core] = jnp.concatenate(kinds, axis=1)


def cut(qkv_weight, out_weight):
    return pl.pallas_call(
        cut_body,
        out_shape=jax.ShapeDtypeStruct((2, out_weight.shape[0], 4 * WIDTH), jnp.bfloat16),
        compiler_params=vmem_params(),
        name="cut",
    )(*[pltpu.with_memory_space_constraint(w, pltpu.HBM) for w in (qkv_weight, out_weight)])


def in_turn(counts_ref, order_ref):
    first, turns = 0, []
    for turn in range(DOCS):
        doc = order_ref[turn]
        turns.append((doc, first, counts_ref[doc]))
        first = first + counts_ref[doc]
    return turns


def rotate_body(where_ref, counts_ref, order_ref, tiles_ref, out_ref, sems):
    start = 0
    for doc, first, _ in in_turn(counts_ref, order_ref):
        start = jnp.where(doc == where_ref[0], first, start)
    copies = [
        pltpu.make_async_copy(
            tiles_ref.at[slot], out_ref.at[(slot + start) & (SLOTS - 1)], sems.at[slot]
        )
        for slot in range(SLOTS)
    ]
    for copy in copies:
        copy.start()
    for copy in copies:
        copy.wait()


def rotate(where, counts, order, tiles):
    in_smem = pl.BlockSpec(memory_space=pltpu.SMEM)
    return pl.pallas_call(
        rotate_body,
        out_shape=jax.ShapeDtypeStruct(tiles.shape, tiles.dtype),
        in_specs=[in_smem, in_smem, in_smem, pl.BlockSpec(memory_space=pl.ANY)],
        out_specs=pl.BlockSpec(memory_space=pltpu.VMEM),
        scratch_shapes=[pltpu.SemaphoreType.DMA((SLOTS,))],
        compiler_params=vmem_params(),
        name="rotate",
    )(where, counts, order, pltpu.with_memory_space_constraint(tiles, pltpu.HBM))


def by_half(rows):
    parts = rows.reshape(ZS, 2, D // (2 * ZS), rows.shape[-1])
    return jnp.concatenate([parts[:, h].reshape(D // 2, rows.shape[-1]) for h in range(2)], axis=0)


def by_z(rows):
    parts = rows.reshape(2, ZS, 1, D // (2 * ZS), rows.shape[-1])
    return jnp.concatenate([parts[0], parts[1]], axis=1).reshape(D, rows.shape[-1])


def normalise_body(where_ref, counts_ref, order_ref, tile_ref, source_ref, normed_ref):
    tile = tile_ref[0]
    source_ref[0] = tile
    values = tile.astype(jnp.float32)
    center = values - jnp.mean(values, axis=0, keepdims=True)
    spread = jnp.mean(center * center, axis=0, keepdims=True)
    normed = by_half(center * lax.rsqrt(spread + EPSILON))
    normed_ref[0] = normed.T.astype(jnp.bfloat16)


def normalise(where, counts, order, arrived):
    def pick(j, where_ref, counts_ref, order_ref):
        packed = where_ref[1] + j * SLOTS
        owner = 0
        for doc, first, count in in_turn(counts_ref, order_ref):
            owner = jnp.where((first <= packed) & (packed < first + count), doc, owner)
        return (owner & 1) * 2 + (owner >> 1), 0, 0

    def same(j, *_):
        return j, 0, 0

    return pl.pallas_call(
        normalise_body,
        out_shape=(
            jax.ShapeDtypeStruct((2, D, PATCH), jnp.bfloat16),
            jax.ShapeDtypeStruct((2, PATCH, D), jnp.bfloat16),
        ),
        grid_spec=pltpu.PrefetchScalarGridSpec(
            num_scalar_prefetch=3,
            grid=(2,),
            in_specs=[pl.BlockSpec((1, D, PATCH), pick)],
            out_specs=(pl.BlockSpec((1, D, PATCH), same), pl.BlockSpec((1, PATCH, D), same)),
        ),
        compiler_params=vmem_params(),
        name="normalise",
    )(where, counts, order, arrived)


def attend(qkv):
    pairs = [(tile, head) for tile in range(4) for head in range(LOCAL)]

    def part(kind, tile, head):
        low = kind * WIDTH + head * HDIM
        return qkv[low : low + HDIM, tile * PATCH : (tile + 1) * PATCH]

    scores = [
        lax.dot_general(
            part(1, *pair), part(0, *pair), (((0,), (0,)), ((), ())),
            preferred_element_type=jnp.float32,
        )
        for pair in pairs
    ]
    scale = HDIM ** (-0.5) * LOG2E
    powers = [jnp.exp2((s - jnp.max(s, axis=0, keepdims=True)) * scale) for s in scores]
    inverse = [1.0 / jnp.sum(p, axis=0, keepdims=True) for p in powers]
    contexts = [
        (
            jnp.dot(part(2, *pair), p.astype(jnp.bfloat16), preferred_element_type=jnp.float32) * i
        ).astype(jnp.bfloat16)
        for pair, p, i in zip(pairs, powers, inverse)
    ]
    return jnp.concatenate(
        [
            jnp.concatenate(contexts[tile * LOCAL : (tile + 1) * LOCAL], axis=0)
            for tile in range(4)
        ],
        axis=1,
    )


def group_contexts(groups, where_ref, own_ref, other_ref, pieces, weight_ref, sems):
    def copies(n, group):
        made = []
        for k in range(PIECES):
            y_hi = ((where_ref[2] + group + k // 2 * GROUPS) >> 2) & 1
            made.append(
                pltpu.make_async_copy(
                    pieces[n * PIECES + k], weight_ref.at[n, y_hi, k % 2], sems.at[n, k]
                )
            )
        return made

    for n, group in enumerate(groups):
        for copy in copies(n, group):
            copy.start()
    normed = jnp.concatenate(
        [ref[...].reshape(2 * PATCH, D) for ref in (own_ref, other_ref)], axis=0
    )
    contexts, outs = [], []
    for n, group in enumerate(groups):
        for copy in copies(n, group):
            copy.wait()
        weight = weight_ref[n].reshape(D, 4 * WIDTH)
        projected = jnp.dot(normed, weight[:, : 3 * WIDTH], preferred_element_type=jnp.float32)
        contexts.append(attend(projected.astype(jnp.bfloat16).T))
        outs.append(weight[:, 3 * WIDTH :])
    return jnp.dot(
        jnp.concatenate(outs, axis=1),
        jnp.concatenate(contexts, axis=0),
        preferred_element_type=jnp.float32,
    )


def early_body(where_ref, own_ref, other_ref, *refs):
    count = len(EARLY) * PIECES
    total_ref, weight_ref, sems = refs[count:]
    total_ref[...] = group_contexts(
        EARLY, where_ref, own_ref, other_ref, refs[:count], weight_ref, sems
    )


def late_body(where_ref, own_ref, other_ref, early_ref, *refs):
    count = len(LATE) * PIECES
    own_out_ref, other_out_ref, weight_ref, sems = refs[count:]
    total = group_contexts(LATE, where_ref, own_ref, other_ref, refs[:count], weight_ref, sems)
    total = by_z(total + early_ref[...])
    for tile in range(4):
        target = (own_out_ref, other_out_ref)[tile // 2]
        target[tile % 2] = total[:, tile * PATCH : (tile + 1) * PATCH].astype(jnp.bfloat16)


def encode(body, groups, out_shape, where, arrays, pieces):
    in_vmem = pl.BlockSpec(memory_space=pltpu.VMEM)
    taken = [pieces[group * PIECES + k] for group in groups for k in range(PIECES)]
    if groups == EARLY:
        taken = [pltpu.with_memory_space_constraint(t, pltpu.HBM) for t in taken]
    flops = 2 * 4 * PATCH * D * 4 * WIDTH * len(groups)
    return pl.pallas_call(
        body,
        out_shape=out_shape,
        in_specs=[pl.BlockSpec(memory_space=pltpu.SMEM)]
        + [in_vmem] * len(arrays)
        + [pl.BlockSpec(memory_space=pl.ANY)] * len(taken),
        out_specs=jax.tree.map(lambda _: in_vmem, out_shape),
        scratch_shapes=[
            pltpu.VMEM((len(groups), 2, 2, D // 4, 4 * WIDTH), jnp.bfloat16),
            pltpu.SemaphoreType.DMA((len(groups), PIECES)),
        ],
        compiler_params=vmem_params(),
        cost_estimate=pl.CostEstimate(
            flops=flops, bytes_accessed=len(groups) * D * 8 * WIDTH, transcendentals=0
        ),
        name=body.__name__,
    )(where, *arrays, *taken)


def around_y(block):
    length = 2 * GROUPS
    half = block.shape[0] // 2
    up = [(i, (i + 1) % length) for i in range(length)]
    down = [(i, (i - 1) % length) for i in range(length)]
    halves = [block[:half], block[half:]]
    rising, falling = list(halves), list(halves)
    found = {(0, 0): halves[0], (0, 1): halves[1]}
    for hop in range(1, length // 2 + 1):
        last = 2 * hop == length
        for k in range(2):
            if not last or k == 0:
                rising[k] = lax.ppermute(rising[k], ("y_hi", "tensor"), up)
                found[length - hop, k] = rising[k]
            if not last or k == 1:
                falling[k] = lax.ppermute(falling[k], ("y_hi", "tensor"), down)
                found[hop, k] = falling[k]
    return [
        found[group + k // 2 * GROUPS, k % 2] for group in range(GROUPS) for k in range(PIECES)
    ]


def local(tiles, tile_counts, doc_order, qkv_weight, out_weight):
    bal_hi, bal_lo = lax.axis_index("bal_hi"), lax.axis_index("bal_lo")
    tensor = lax.axis_index("tensor")
    swap = [(0, 1), (1, 0)]

    place = bal_lo * 8 + bal_hi * 4 + tensor
    y = lax.axis_index("y_hi") * 4 + tensor
    where = jnp.stack([bal_hi * 2 + bal_lo, place, y]).astype(jnp.int32)
    counts, order = tile_counts[0], doc_order[0]

    halves = cut(qkv_weight, out_weight)
    both = lax.all_to_all(halves, "core", 0, 0, tiled=True).reshape(-1, 4 * WIDTH)

    outbound = rotate(where, counts, order, tiles[0, 0])
    outbound, both = lax.optimization_barrier((outbound, both))
    arrived = lax.all_to_all(outbound, ("bal_lo", "bal_hi", "tensor"), 0, 0, tiled=True)
    block = lax.all_gather(both, "z", axis=0, tiled=True)
    pieces = around_y(block)
    source, normed = normalise(where, counts, order, arrived.reshape(4, D, PATCH))
    other = lax.ppermute(normed, "core", swap)

    early = jax.ShapeDtypeStruct((D, 4 * PATCH), jnp.float32)
    part = jax.ShapeDtypeStruct((2, D, PATCH), jnp.bfloat16)
    total = encode(early_body, EARLY, early, where, (normed, other), pieces)
    own_part, other_part = encode(
        late_body, LATE, (part, part), where, (normed, other, total), pieces
    )
    back_part = lax.ppermute(other_part, "core", swap)
    encoded = (
        source.astype(jnp.float32) + own_part.astype(jnp.float32) + back_part.astype(jnp.float32)
    ).astype(jnp.bfloat16)
    returned = lax.all_to_all(
        encoded.reshape(8, D // 4, PATCH), ("bal_hi", "tensor"), 0, 0, tiled=True
    )
    return returned[None]


def solution(mesh):
    z = mesh.shape["dp"] // 4
    devices = mesh.devices.reshape(z, 2, 2, 2, 2, 4)
    fine = Mesh(devices, ("z", "y_hi", "core", "bal_hi", "bal_lo", "tensor"))
    dp, bal = ("z", "y_hi", "core"), ("bal_hi", "bal_lo")
    placed = (
        P(dp, bal, None, "tensor", None),
        P(dp, None),
        P(dp, None),
        P(None, dp, "tensor"),
        P(dp, "tensor"),
    )
    return jax.shard_map(
        local, mesh=fine, in_specs=placed, out_specs=P(dp, bal, "tensor", None), check_vma=False
    )
```

```python
import jax
import jax.numpy as jnp
from jax import lax
from jax.experimental import pallas as pl
from jax.experimental.pallas import tpu as pltpu
from jax.sharding import Mesh, PartitionSpec as P

D = 1280
HDIM = 80
PATCH = 128
SLOTS = 16
DOCS = 4
ZS = 16
GROUPS = 4
PIECES = 3
EARLY, LATE = (2, 1, 3), (0,)
LOCAL = 2
WIDTH = LOCAL * HDIM
EPSILON = 1e-06
VMEM = 32 * 2**20
LOG2E = 1.4426950408889634


def vmem_params():
    return pltpu.CompilerParams(vmem_limit_bytes=VMEM)


def cut_body(qkv_ref, out_ref, halves_ref):
    for core in range(2):
        low = core * WIDTH
        kinds = [qkv_ref[k, :, low : low + WIDTH] for k in range(3)] + [out_ref[:, low : low + WIDTH]]
        halves_ref[core] = jnp.concatenate(kinds, axis=1)


def cut(qkv_weight, out_weight):
    return pl.pallas_call(
        cut_body,
        out_shape=jax.ShapeDtypeStruct((2, out_weight.shape[0], 4 * WIDTH), jnp.bfloat16),
        compiler_params=vmem_params(),
        name="cut",
    )(*[pltpu.with_memory_space_constraint(w, pltpu.HBM) for w in (qkv_weight, out_weight)])


def in_turn(counts_ref, order_ref):
    first, turns = 0, []
    for turn in range(DOCS):
        doc = order_ref[turn]
        turns.append((doc, first, counts_ref[doc]))
        first = first + counts_ref[doc]
    return turns


def rotate_body(where_ref, counts_ref, order_ref, tiles_ref, out_ref, sems):
    start = 0
    for doc, first, _ in in_turn(counts_ref, order_ref):
        start = jnp.where(doc == where_ref[0], first, start)
    copies = [
        pltpu.make_async_copy(
            tiles_ref.at[slot], out_ref.at[(slot + start) & (SLOTS - 1)], sems.at[slot]
        )
        for slot in range(SLOTS)
    ]
    for copy in copies:
        copy.start()
    for copy in copies:
        copy.wait()


def rotate(where, counts, order, tiles):
    in_smem = pl.BlockSpec(memory_space=pltpu.SMEM)
    return pl.pallas_call(
        rotate_body,
        out_shape=jax.ShapeDtypeStruct(tiles.shape, tiles.dtype),
        in_specs=[in_smem, in_smem, in_smem, pl.BlockSpec(memory_space=pl.ANY)],
        out_specs=pl.BlockSpec(memory_space=pltpu.VMEM),
        scratch_shapes=[pltpu.SemaphoreType.DMA((SLOTS,))],
        compiler_params=vmem_params(),
        name="rotate",
    )(where, counts, order, pltpu.with_memory_space_constraint(tiles, pltpu.HBM))


def by_half(rows):
    parts = rows.reshape(ZS, 2, D // (2 * ZS), rows.shape[-1])
    return jnp.concatenate([parts[:, h].reshape(D // 2, rows.shape[-1]) for h in range(2)], axis=0)


def by_z(rows):
    parts = rows.reshape(2, ZS, 1, D // (2 * ZS), rows.shape[-1])
    return jnp.concatenate([parts[0], parts[1]], axis=1).reshape(D, rows.shape[-1])


def normalise_body(where_ref, counts_ref, order_ref, tile_ref, source_ref, normed_ref):
    tile = tile_ref[0]
    source_ref[0] = tile
    values = tile.astype(jnp.float32)
    center = values - jnp.mean(values, axis=0, keepdims=True)
    spread = jnp.mean(center * center, axis=0, keepdims=True)
    normed = by_half(center * lax.rsqrt(spread + EPSILON))
    normed_ref[0] = normed.T.astype(jnp.bfloat16)


def normalise(where, counts, order, arrived):
    def pick(j, where_ref, counts_ref, order_ref):
        packed = where_ref[1] + j * SLOTS
        owner = 0
        for doc, first, count in in_turn(counts_ref, order_ref):
            owner = jnp.where((first <= packed) & (packed < first + count), doc, owner)
        return (owner & 1) * 2 + (owner >> 1), 0, 0

    def same(j, *_):
        return j, 0, 0

    return pl.pallas_call(
        normalise_body,
        out_shape=(
            jax.ShapeDtypeStruct((2, D, PATCH), jnp.bfloat16),
            jax.ShapeDtypeStruct((2, PATCH, D), jnp.bfloat16),
        ),
        grid_spec=pltpu.PrefetchScalarGridSpec(
            num_scalar_prefetch=3,
            grid=(2,),
            in_specs=[pl.BlockSpec((1, D, PATCH), pick)],
            out_specs=(pl.BlockSpec((1, D, PATCH), same), pl.BlockSpec((1, PATCH, D), same)),
        ),
        compiler_params=vmem_params(),
        name="normalise",
    )(where, counts, order, arrived)


def attend(qkv):
    pairs = [(tile, head) for tile in range(4) for head in range(LOCAL)]

    def part(kind, tile, head):
        low = kind * WIDTH + head * HDIM
        return qkv[low : low + HDIM, tile * PATCH : (tile + 1) * PATCH]

    scores = [
        lax.dot_general(
            part(1, *pair), part(0, *pair), (((0,), (0,)), ((), ())),
            preferred_element_type=jnp.float32,
        )
        for pair in pairs
    ]
    scale = HDIM ** (-0.5) * LOG2E
    powers = [jnp.exp2((s - jnp.max(s, axis=0, keepdims=True)) * scale) for s in scores]
    inverse = [1.0 / jnp.sum(p, axis=0, keepdims=True) for p in powers]
    contexts = [
        (
            jnp.dot(part(2, *pair), p.astype(jnp.bfloat16), preferred_element_type=jnp.float32) * i
        ).astype(jnp.bfloat16)
        for pair, p, i in zip(pairs, powers, inverse)
    ]
    return jnp.concatenate(
        [
            jnp.concatenate(contexts[tile * LOCAL : (tile + 1) * LOCAL], axis=0)
            for tile in range(4)
        ],
        axis=1,
    )


def group_contexts(groups, where_ref, own_ref, other_ref, pieces, weight_ref, sems):
    half = D // 4
    taken = iter(pieces)
    copies = []
    for n, group in enumerate(groups):
        parts = []
        for k in range(2):
            y_hi = ((where_ref[2] + where_ref[3] * (group + k * GROUPS)) >> 2) & 1
            target = weight_ref.at[n, y_hi]
            if group + k * GROUPS == GROUPS:
                targets = [target.at[pl.ds(0, half)], target.at[pl.ds(half, half)]]
            else:
                targets = [target]
            for t in targets:
                parts.append(pltpu.make_async_copy(next(taken), t, sems.at[n, len(parts)]))
        copies.append(parts)
    for parts in copies:
        for copy in parts:
            copy.start()
    normed = jnp.concatenate(
        [ref[...].reshape(2 * PATCH, D) for ref in (own_ref, other_ref)], axis=0
    )
    contexts, outs = [], []
    for n, parts in enumerate(copies):
        for copy in parts:
            copy.wait()
        weight = weight_ref[n].reshape(D, 4 * WIDTH)
        projected = jnp.dot(normed, weight[:, : 3 * WIDTH], preferred_element_type=jnp.float32)
        contexts.append(attend(projected.astype(jnp.bfloat16).T))
        outs.append(weight[:, 3 * WIDTH :])
    return jnp.dot(
        jnp.concatenate(outs, axis=1),
        jnp.concatenate(contexts, axis=0),
        preferred_element_type=jnp.float32,
    )


def early_body(where_ref, own_ref, other_ref, *refs):
    total_ref, weight_ref, sems = refs[-3:]
    total_ref[...] = group_contexts(
        EARLY, where_ref, own_ref, other_ref, refs[:-3], weight_ref, sems
    )


def late_body(where_ref, own_ref, other_ref, early_ref, *refs):
    outs, (weight_ref, sems) = refs[-4:-2], refs[-2:]
    total = group_contexts(LATE, where_ref, own_ref, other_ref, refs[:-4], weight_ref, sems)
    total = by_z(total + early_ref[...])
    for tile in range(4):
        block = total[:, tile * PATCH : (tile + 1) * PATCH]
        outs[tile // 2][tile % 2] = block.astype(jnp.bfloat16)


def encode(body, groups, out_shape, where, arrays, pieces):
    in_vmem = pl.BlockSpec(memory_space=pltpu.VMEM)
    keys = [group + k * GROUPS for group in groups for k in range(2)]
    taken = [pieces[key] for key in keys if key != GROUPS]
    if GROUPS in keys:
        taken += [pieces[GROUPS, 0], pieces[GROUPS, 1]]
    if groups == EARLY:
        taken = [pltpu.with_memory_space_constraint(t, pltpu.HBM) for t in taken]
    flops = 2 * 4 * PATCH * D * 4 * WIDTH * len(groups)
    return pl.pallas_call(
        body,
        out_shape=out_shape,
        in_specs=[pl.BlockSpec(memory_space=pltpu.SMEM)]
        + [in_vmem] * len(arrays)
        + [pl.BlockSpec(memory_space=pl.ANY)] * len(taken),
        out_specs=jax.tree.map(lambda _: in_vmem, out_shape),
        scratch_shapes=[
            pltpu.VMEM((len(groups), 2, D // 2, 4 * WIDTH), jnp.bfloat16),
            pltpu.SemaphoreType.DMA((len(groups), PIECES)),
        ],
        compiler_params=vmem_params(),
        cost_estimate=pl.CostEstimate(
            flops=flops, bytes_accessed=len(groups) * D * 8 * WIDTH, transcendentals=0
        ),
        name=body.__name__,
    )(where, *arrays, *taken)


def around_y(block):
    length = 2 * GROUPS

    def ways(chain):
        pairs = []
        for y in range(length):
            for core in range(2):
                to = (y + (1 if core == chain else -1)) % length
                pairs.append(tuple(p // 4 * 8 + core * 4 + p % 4 for p in (y, to)))
        return pairs

    held = [block, block]
    found = {0: block}
    for hop in range(1, length // 2 + 1):
        for chain in range(2):
            if 2 * hop == length:
                half = block.shape[0] // 2
                held[chain] = held[chain][chain * half : (chain + 1) * half]
            held[chain] = lax.ppermute(held[chain], ("y_hi", "core", "tensor"), ways(chain))
            found[(hop if chain else -hop) % length if 2 * hop < length else (hop, chain)] = held[chain]
    return found


def local(tiles, tile_counts, doc_order, qkv_weight, out_weight):
    bal_hi, bal_lo = lax.axis_index("bal_hi"), lax.axis_index("bal_lo")
    tensor = lax.axis_index("tensor")
    swap = [(0, 1), (1, 0)]

    place = bal_lo * 8 + bal_hi * 4 + tensor
    y = lax.axis_index("y_hi") * 4 + tensor
    along = 1 - 2 * lax.axis_index("core")
    where = jnp.stack([bal_hi * 2 + bal_lo, place, y, along]).astype(jnp.int32)
    counts, order = tile_counts[0], doc_order[0]

    halves = cut(qkv_weight, out_weight)
    both = lax.all_to_all(halves, "core", 0, 0, tiled=True).reshape(-1, 4 * WIDTH)

    outbound = rotate(where, counts, order, tiles[0, 0])
    outbound, both = lax.optimization_barrier((outbound, both))
    arrived = lax.all_to_all(outbound, ("bal_lo", "bal_hi", "tensor"), 0, 0, tiled=True)
    block = lax.all_gather(both, "z", axis=0, tiled=True)
    pieces = around_y(block)
    source, normed = normalise(where, counts, order, arrived.reshape(4, D, PATCH))
    other = lax.ppermute(normed, "core", swap)

    early = jax.ShapeDtypeStruct((D, 4 * PATCH), jnp.float32)
    part = jax.ShapeDtypeStruct((2, D, PATCH), jnp.bfloat16)
    total = encode(early_body, EARLY, early, where, (normed, other), pieces)
    own_part, other_part = encode(
        late_body, LATE, (part, part), where, (normed, other, total), pieces
    )
    back_part = lax.ppermute(other_part, "core", swap)
    encoded = sum(a.astype(jnp.float32) for a in (source, own_part, back_part))
    encoded = encoded.astype(jnp.bfloat16).reshape(8, D // 4, PATCH)
    return lax.all_to_all(encoded, ("bal_hi", "tensor"), 0, 0, tiled=True)[None]


def solution(mesh):
    z = mesh.shape["dp"] // 4
    devices = mesh.devices.reshape(z, 2, 2, 2, 2, 4)
    fine = Mesh(devices, ("z", "y_hi", "core", "bal_hi", "bal_lo", "tensor"))
    dp, bal = ("z", "y_hi", "core"), ("bal_hi", "bal_lo")
    placed = (
        P(dp, bal, None, "tensor", None),
        P(dp, None),
        P(dp, None),
        P(None, dp, "tensor"),
        P(dp, "tensor"),
    )
    return jax.shard_map(
        local, mesh=fine, in_specs=placed, out_specs=P(dp, bal, "tensor", None), check_vma=False
    )
```

```python
import jax
import jax.numpy as jnp
from jax import lax
from jax.experimental import pallas as pl
from jax.experimental.pallas import tpu as pltpu
from jax.sharding import Mesh, PartitionSpec as P

D = 1280
HDIM = 80
PATCH = 128
SLOTS = 16
DOCS = 4
BAL, PLACE, RING, CORE, COUNTS, ORDER = 0, 1, 2, 3, 4, 4 + DOCS
ZS = 16
GROUPS = 4
PIECES = 4
EARLY, LATE = (2, 1, 3), (0,)
LOCAL = 2
WIDTH = LOCAL * HDIM
EPSILON = 1e-06
VMEM = 32 * 2**20
LOG2E = 1.4426950408889634


def vmem_params():
    return pltpu.CompilerParams(vmem_limit_bytes=VMEM)


def cut_body(facts_ref, qkv_ref, out_ref, keep_ref, send_ref):
    halves = []
    for core in range(2):
        low = core * WIDTH
        kinds = [qkv_ref[k, :, low : low + WIDTH] for k in range(3)] + [out_ref[:, low : low + WIDTH]]
        halves.append(jnp.concatenate(kinds, axis=1))

    def put(keep, send):
        keep_ref[...] = halves[keep]
        send_ref[...] = halves[send]

    pl.when(facts_ref[CORE] == 0)(lambda: put(0, 1))
    pl.when(facts_ref[CORE] != 0)(lambda: put(1, 0))


def cut(facts, qkv_weight, out_weight):
    in_vmem = pl.BlockSpec(memory_space=pltpu.VMEM)
    half = jax.ShapeDtypeStruct((out_weight.shape[0], 4 * WIDTH), jnp.bfloat16)
    return pl.pallas_call(
        cut_body,
        out_shape=(half, half),
        in_specs=[pl.BlockSpec(memory_space=pltpu.SMEM), in_vmem, in_vmem],
        out_specs=(in_vmem, in_vmem),
        compiler_params=vmem_params(),
        name="cut",
    )(facts, *[pltpu.with_memory_space_constraint(w, pltpu.HBM) for w in (qkv_weight, out_weight)])


def in_turn(facts_ref):
    first, turns = 0, []
    for turn in range(DOCS):
        doc = facts_ref[ORDER + turn]
        count = facts_ref[COUNTS + doc]
        turns.append((doc, first, count))
        first = first + count
    return turns


def rotate_body(facts_ref, tiles_ref, out_ref, held_ref, in_sems, out_sems):
    start = 0
    for doc, first, _ in in_turn(facts_ref):
        start = jnp.where(doc == facts_ref[BAL], first, start)
    arriving = [
        pltpu.make_async_copy(tiles_ref.at[slot], held_ref.at[slot], in_sems.at[slot])
        for slot in range(SLOTS)
    ]
    leaving = [
        pltpu.make_async_copy(
            held_ref.at[slot], out_ref.at[(slot + start) & (SLOTS - 1)], out_sems.at[slot]
        )
        for slot in range(SLOTS)
    ]
    for copy in arriving:
        copy.start()
    for slot in range(SLOTS):
        arriving[slot].wait()
        leaving[slot].start()
    for copy in leaving:
        copy.wait()


def rotate(facts, tiles):
    return pl.pallas_call(
        rotate_body,
        out_shape=jax.ShapeDtypeStruct(tiles.shape, tiles.dtype),
        in_specs=[pl.BlockSpec(memory_space=pltpu.SMEM), pl.BlockSpec(memory_space=pl.ANY)],
        out_specs=pl.BlockSpec(memory_space=pl.ANY),
        scratch_shapes=[
            pltpu.VMEM(tiles.shape, tiles.dtype),
            pltpu.SemaphoreType.DMA((SLOTS,)),
            pltpu.SemaphoreType.DMA((SLOTS,)),
        ],
        compiler_params=vmem_params(),
        name="rotate",
    )(facts, pltpu.with_memory_space_constraint(tiles, pltpu.HBM))


def by_half(rows):
    parts = rows.reshape(ZS, 2, D // (2 * ZS), rows.shape[-1])
    return jnp.concatenate([parts[:, h].reshape(D // 2, rows.shape[-1]) for h in range(2)], axis=0)


def by_z(rows):
    parts = rows.reshape(2, ZS, 1, D // (2 * ZS), rows.shape[-1])
    return jnp.concatenate([parts[0], parts[1]], axis=1).reshape(D, rows.shape[-1])


def normalise_body(facts_ref, tile_ref, source_ref, normed_ref):
    tile = tile_ref[0]
    source_ref[0] = tile
    values = tile.astype(jnp.float32)
    center = values - jnp.mean(values, axis=0, keepdims=True)
    spread = jnp.mean(center * center, axis=0, keepdims=True)
    normed = by_half(center * lax.rsqrt(spread + EPSILON))
    normed_ref[0] = normed.T.astype(jnp.bfloat16)


def normalise(facts, arrived):
    def pick(j, facts_ref):
        packed = facts_ref[PLACE] + j * SLOTS
        owner = 0
        for doc, first, count in in_turn(facts_ref):
            owner = jnp.where((first <= packed) & (packed < first + count), doc, owner)
        return (owner & 1) * 2 + (owner >> 1), 0, 0

    def same(j, *_):
        return j, 0, 0

    return pl.pallas_call(
        normalise_body,
        out_shape=(
            jax.ShapeDtypeStruct((2, D, PATCH), jnp.bfloat16),
            jax.ShapeDtypeStruct((2, PATCH, D), jnp.bfloat16),
        ),
        grid_spec=pltpu.PrefetchScalarGridSpec(
            num_scalar_prefetch=1,
            grid=(2,),
            in_specs=[pl.BlockSpec((1, D, PATCH), pick)],
            out_specs=(pl.BlockSpec((1, D, PATCH), same), pl.BlockSpec((1, PATCH, D), same)),
        ),
        compiler_params=vmem_params(),
        name="normalise",
    )(facts, arrived)


def attend(qkv):
    pairs = [(tile, head) for tile in range(4) for head in range(LOCAL)]

    def part(kind, tile, head):
        low = kind * WIDTH + head * HDIM
        return qkv[low : low + HDIM, tile * PATCH : (tile + 1) * PATCH]

    scores = [
        lax.dot_general(
            part(1, *pair), part(0, *pair), (((0,), (0,)), ((), ())),
            preferred_element_type=jnp.float32,
        )
        for pair in pairs
    ]
    scale = HDIM ** (-0.5) * LOG2E
    powers = [jnp.exp2((s - jnp.max(s, axis=0, keepdims=True)) * scale) for s in scores]
    inverse = [1.0 / jnp.sum(p, axis=0, keepdims=True) for p in powers]
    contexts = [
        (
            jnp.dot(part(2, *pair), p.astype(jnp.bfloat16), preferred_element_type=jnp.float32) * i
        ).astype(jnp.bfloat16)
        for pair, p, i in zip(pairs, powers, inverse)
    ]
    return jnp.concatenate(
        [
            jnp.concatenate(contexts[tile * LOCAL : (tile + 1) * LOCAL], axis=0)
            for tile in range(4)
        ],
        axis=1,
    )


def group_contexts(groups, facts_ref, own_ref, other_ref, pieces, weight_ref, sems):
    def copies(n, group):
        made = []
        for k in range(PIECES):
            y_hi = ((facts_ref[RING] + group + k // 2 * GROUPS) >> 2) & 1
            made.append(
                pltpu.make_async_copy(
                    pieces[n * PIECES + k], weight_ref.at[n, y_hi, k % 2], sems.at[n, k]
                )
            )
        return made

    for n, group in enumerate(groups):
        for copy in copies(n, group):
            copy.start()
    normed = jnp.concatenate(
        [ref[...].reshape(2 * PATCH, D) for ref in (own_ref, other_ref)], axis=0
    )
    contexts, outs = [], []
    for n, group in enumerate(groups):
        for copy in copies(n, group):
            copy.wait()
        weight = weight_ref[n].reshape(D, 4 * WIDTH)
        projected = jnp.dot(normed, weight[:, : 3 * WIDTH], preferred_element_type=jnp.float32)
        contexts.append(attend(projected.astype(jnp.bfloat16).T))
        outs.append(weight[:, 3 * WIDTH :])
    return jnp.dot(
        jnp.concatenate(outs, axis=1),
        jnp.concatenate(contexts, axis=0),
        preferred_element_type=jnp.float32,
    )


def early_body(facts_ref, own_ref, other_ref, *refs):
    count = len(EARLY) * PIECES
    total_ref, weight_ref, sems = refs[count:]
    total_ref[...] = group_contexts(
        EARLY, facts_ref, own_ref, other_ref, refs[:count], weight_ref, sems
    )


def late_body(facts_ref, own_ref, other_ref, early_ref, *refs):
    count = len(LATE) * PIECES
    own_out_ref, other_out_ref, weight_ref, sems = refs[count:]
    total = group_contexts(LATE, facts_ref, own_ref, other_ref, refs[:count], weight_ref, sems)
    total = by_z(total + early_ref[...])
    for tile in range(4):
        target = (own_out_ref, other_out_ref)[tile // 2]
        target[tile % 2] = total[:, tile * PATCH : (tile + 1) * PATCH].astype(jnp.bfloat16)


def encode(body, groups, out_shape, facts, arrays, pieces):
    in_vmem = pl.BlockSpec(memory_space=pltpu.VMEM)
    taken = [pieces[group * PIECES + k] for group in groups for k in range(PIECES)]
    if groups == EARLY:
        taken = [pltpu.with_memory_space_constraint(t, pltpu.HBM) for t in taken]
    flops = 2 * 4 * PATCH * D * 4 * WIDTH * len(groups)
    return pl.pallas_call(
        body,
        out_shape=out_shape,
        in_specs=[pl.BlockSpec(memory_space=pltpu.SMEM)]
        + [in_vmem] * len(arrays)
        + [pl.BlockSpec(memory_space=pl.ANY)] * len(taken),
        out_specs=jax.tree.map(lambda _: in_vmem, out_shape),
        scratch_shapes=[
            pltpu.VMEM((len(groups), 2, 2, D // 4, 4 * WIDTH), jnp.bfloat16),
            pltpu.SemaphoreType.DMA((len(groups), PIECES)),
        ],
        compiler_params=vmem_params(),
        cost_estimate=pl.CostEstimate(
            flops=flops, bytes_accessed=len(groups) * D * 8 * WIDTH, transcendentals=0
        ),
        name=body.__name__,
    )(facts, *arrays, *taken)


def around_y(block):
    length = 2 * GROUPS
    half = block.shape[0] // 2
    up = [(i, (i + 1) % length) for i in range(length)]
    down = [(i, (i - 1) % length) for i in range(length)]
    halves = [block[:half], block[half:]]
    rising, falling = list(halves), list(halves)
    found = {(0, 0): halves[0], (0, 1): halves[1]}
    for hop in range(1, length // 2 + 1):
        last = 2 * hop == length
        for k in range(2):
            if not last or k == 0:
                rising[k] = lax.ppermute(rising[k], ("y_hi", "tensor"), up)
                found[length - hop, k] = rising[k]
            if not last or k == 1:
                falling[k] = lax.ppermute(falling[k], ("y_hi", "tensor"), down)
                found[hop, k] = falling[k]
    return [
        found[group + k // 2 * GROUPS, k % 2] for group in range(GROUPS) for k in range(PIECES)
    ]


def local(tiles, tile_counts, doc_order, qkv_weight, out_weight):
    bal_hi, bal_lo = lax.axis_index("bal_hi"), lax.axis_index("bal_lo")
    tensor = lax.axis_index("tensor")
    swap = [(0, 1), (1, 0)]

    place = bal_lo * 8 + bal_hi * 4 + tensor
    y = lax.axis_index("y_hi") * 4 + tensor
    core = lax.axis_index("core")
    here = jnp.stack([bal_hi * 2 + bal_lo, place, y, core]).astype(jnp.int32)
    facts = jnp.concatenate([here, tile_counts[0], doc_order[0]])

    outbound = rotate(facts, tiles[0, 0])
    outbound, qkv_weight, out_weight = lax.optimization_barrier((outbound, qkv_weight, out_weight))
    arrived = lax.all_to_all(outbound, ("bal_lo", "bal_hi", "tensor"), 0, 0, tiled=True)

    keep, send = cut(facts, qkv_weight, out_weight)
    got = lax.ppermute(send, "core", swap)
    first, second = jnp.where(core == 0, keep, got), jnp.where(core == 0, got, keep)
    both = jnp.concatenate([first, second])
    block = lax.all_gather(both, "z", axis=0, tiled=True)
    pieces = around_y(block)
    source, normed = normalise(facts, arrived.reshape(4, D, PATCH))
    other = lax.ppermute(normed, "core", swap)

    early = jax.ShapeDtypeStruct((D, 4 * PATCH), jnp.float32)
    part = jax.ShapeDtypeStruct((2, D, PATCH), jnp.bfloat16)
    total = encode(early_body, EARLY, early, facts, (normed, other), pieces)
    own_part, other_part = encode(
        late_body, LATE, (part, part), facts, (normed, other, total), pieces
    )
    back_part = lax.ppermute(other_part, "core", swap)
    encoded = (
        source.astype(jnp.float32) + own_part.astype(jnp.float32) + back_part.astype(jnp.float32)
    ).astype(jnp.bfloat16)
    returned = lax.all_to_all(
        encoded.reshape(8, D // 4, PATCH), ("bal_hi", "tensor"), 0, 0, tiled=True
    )
    return returned[None]


def solution(mesh):
    z = mesh.shape["dp"] // 4
    devices = mesh.devices.reshape(z, 2, 2, 2, 2, 4)
    fine = Mesh(devices, ("z", "y_hi", "core", "bal_hi", "bal_lo", "tensor"))
    dp, bal = ("z", "y_hi", "core"), ("bal_hi", "bal_lo")
    placed = (
        P(dp, bal, None, "tensor", None),
        P(dp, None),
        P(dp, None),
        P(None, dp, "tensor"),
        P(dp, "tensor"),
    )
    return jax.shard_map(
        local, mesh=fine, in_specs=placed, out_specs=P(dp, bal, "tensor", None), check_vma=False
    )
```

```python
import jax
import jax.numpy as jnp
from jax import lax
from jax.experimental import pallas as pl
from jax.experimental.pallas import tpu as pltpu
from jax.sharding import Mesh, PartitionSpec as P

D = 1280
HDIM = 80
PATCH = 128
SLOTS = 16
DOCS = 4
BAL, PLACE, RING, CORE, COUNTS, ORDER = 0, 1, 2, 3, 4, 4 + DOCS
ZS = 16
GROUPS = 4
PIECES = 4
EARLY, LATE = (2, 1, 3), (0,)
LOCAL = 2
WIDTH = LOCAL * HDIM
EPSILON = 1e-06
VMEM = 32 * 2**20
LOG2E = 1.4426950408889634


def vmem_params():
    return pltpu.CompilerParams(vmem_limit_bytes=VMEM)


def cut_body(facts_ref, qkv_ref, out_ref, keep_ref, send_ref):
    halves = []
    for core in range(2):
        low = core * WIDTH
        kinds = [qkv_ref[k, :, low : low + WIDTH] for k in range(3)] + [out_ref[:, low : low + WIDTH]]
        halves.append(jnp.concatenate(kinds, axis=1))

    def put(keep, send):
        keep_ref[...] = halves[keep]
        send_ref[...] = halves[send]

    pl.when(facts_ref[CORE] == 0)(lambda: put(0, 1))
    pl.when(facts_ref[CORE] != 0)(lambda: put(1, 0))


def cut(facts, qkv_weight, out_weight):
    in_vmem = pl.BlockSpec(memory_space=pltpu.VMEM)
    half = jax.ShapeDtypeStruct((out_weight.shape[0], 4 * WIDTH), jnp.bfloat16)
    return pl.pallas_call(
        cut_body,
        out_shape=(half, half),
        in_specs=[pl.BlockSpec(memory_space=pltpu.SMEM), in_vmem, in_vmem],
        out_specs=(in_vmem, in_vmem),
        compiler_params=vmem_params(),
        name="cut",
    )(facts, *[pltpu.with_memory_space_constraint(w, pltpu.HBM) for w in (qkv_weight, out_weight)])


def in_turn(facts_ref):
    first, turns = 0, []
    for turn in range(DOCS):
        doc = facts_ref[ORDER + turn]
        count = facts_ref[COUNTS + doc]
        turns.append((doc, first, count))
        first = first + count
    return turns


def rotate_body(facts_ref, tiles_ref, out_ref, held_ref, in_sems, out_sems):
    start = 0
    for doc, first, _ in in_turn(facts_ref):
        start = jnp.where(doc == facts_ref[BAL], first, start)
    arriving = [
        pltpu.make_async_copy(tiles_ref.at[slot], held_ref.at[slot], in_sems.at[slot])
        for slot in range(SLOTS)
    ]
    leaving = [
        pltpu.make_async_copy(
            held_ref.at[slot], out_ref.at[(slot + start) & (SLOTS - 1)], out_sems.at[slot]
        )
        for slot in range(SLOTS)
    ]
    for copy in arriving:
        copy.start()
    for slot in range(SLOTS):
        arriving[slot].wait()
        leaving[slot].start()
    for copy in leaving:
        copy.wait()


def rotate(facts, tiles):
    return pl.pallas_call(
        rotate_body,
        out_shape=jax.ShapeDtypeStruct(tiles.shape, tiles.dtype),
        in_specs=[pl.BlockSpec(memory_space=pltpu.SMEM), pl.BlockSpec(memory_space=pl.ANY)],
        out_specs=pl.BlockSpec(memory_space=pl.ANY),
        scratch_shapes=[
            pltpu.VMEM(tiles.shape, tiles.dtype),
            pltpu.SemaphoreType.DMA((SLOTS,)),
            pltpu.SemaphoreType.DMA((SLOTS,)),
        ],
        compiler_params=vmem_params(),
        name="rotate",
    )(facts, pltpu.with_memory_space_constraint(tiles, pltpu.HBM))


def by_half(rows):
    parts = rows.reshape(ZS, 2, D // (2 * ZS), rows.shape[-1])
    return jnp.concatenate([parts[:, h].reshape(D // 2, rows.shape[-1]) for h in range(2)], axis=0)


def by_z(rows):
    parts = rows.reshape(2, ZS, 1, D // (2 * ZS), rows.shape[-1])
    return jnp.concatenate([parts[0], parts[1]], axis=1).reshape(D, rows.shape[-1])


def normalise_body(facts_ref, tile_ref, source_ref, normed_ref):
    tile = tile_ref[0]
    source_ref[0] = tile
    values = tile.astype(jnp.float32)
    center = values - jnp.mean(values, axis=0, keepdims=True)
    spread = jnp.mean(center * center, axis=0, keepdims=True)
    normed = by_half(center * lax.rsqrt(spread + EPSILON))
    normed_ref[0] = normed.T.astype(jnp.bfloat16)


def normalise(facts, arrived):
    def pick(j, facts_ref):
        packed = facts_ref[PLACE] + j * SLOTS
        owner = 0
        for doc, first, count in in_turn(facts_ref):
            owner = jnp.where((first <= packed) & (packed < first + count), doc, owner)
        return (owner & 1) * 2 + (owner >> 1), 0, 0

    def same(j, *_):
        return j, 0, 0

    return pl.pallas_call(
        normalise_body,
        out_shape=(
            jax.ShapeDtypeStruct((2, D, PATCH), jnp.bfloat16),
            jax.ShapeDtypeStruct((2, PATCH, D), jnp.bfloat16),
        ),
        grid_spec=pltpu.PrefetchScalarGridSpec(
            num_scalar_prefetch=1,
            grid=(2,),
            in_specs=[pl.BlockSpec((1, D, PATCH), pick)],
            out_specs=(pl.BlockSpec((1, D, PATCH), same), pl.BlockSpec((1, PATCH, D), same)),
        ),
        compiler_params=vmem_params(),
        name="normalise",
    )(facts, arrived)


def attend(qkv):
    pairs = [(tile, head) for tile in range(4) for head in range(LOCAL)]

    def part(kind, tile, head):
        low = kind * WIDTH + head * HDIM
        return qkv[low : low + HDIM, tile * PATCH : (tile + 1) * PATCH]

    scores = [
        lax.dot_general(
            part(1, *pair), part(0, *pair), (((0,), (0,)), ((), ())),
            preferred_element_type=jnp.float32,
        )
        for pair in pairs
    ]
    scale = HDIM ** (-0.5) * LOG2E
    powers = [jnp.exp2((s - jnp.max(s, axis=0, keepdims=True)) * scale) for s in scores]
    inverse = [1.0 / jnp.sum(p, axis=0, keepdims=True) for p in powers]
    contexts = [
        (
            jnp.dot(part(2, *pair), p.astype(jnp.bfloat16), preferred_element_type=jnp.float32) * i
        ).astype(jnp.bfloat16)
        for pair, p, i in zip(pairs, powers, inverse)
    ]
    return jnp.concatenate(
        [
            jnp.concatenate(contexts[tile * LOCAL : (tile + 1) * LOCAL], axis=0)
            for tile in range(4)
        ],
        axis=1,
    )


def group_contexts(groups, facts_ref, own_ref, other_ref, pieces, weight_ref, sems):
    def copies(n, group):
        made = []
        for k in range(PIECES):
            away = (1 - 2 * facts_ref[CORE]) * (group + k // 2 * GROUPS)
            y_hi = ((facts_ref[RING] + away) >> 2) & 1
            made.append(
                pltpu.make_async_copy(
                    pieces[n * PIECES + k], weight_ref.at[n, y_hi, k % 2], sems.at[n, k]
                )
            )
        return made

    for n, group in enumerate(groups):
        for copy in copies(n, group):
            copy.start()
    normed = jnp.concatenate(
        [ref[...].reshape(2 * PATCH, D) for ref in (own_ref, other_ref)], axis=0
    )
    contexts, outs = [], []
    for n, group in enumerate(groups):
        for copy in copies(n, group):
            copy.wait()
        weight = weight_ref[n].reshape(D, 4 * WIDTH)
        projected = jnp.dot(normed, weight[:, : 3 * WIDTH], preferred_element_type=jnp.float32)
        contexts.append(attend(projected.astype(jnp.bfloat16).T))
        outs.append(weight[:, 3 * WIDTH :])
    return jnp.dot(
        jnp.concatenate(outs, axis=1),
        jnp.concatenate(contexts, axis=0),
        preferred_element_type=jnp.float32,
    )


def early_body(facts_ref, own_ref, other_ref, *refs):
    count = len(EARLY) * PIECES
    total_ref, weight_ref, sems = refs[count:]
    total_ref[...] = group_contexts(
        EARLY, facts_ref, own_ref, other_ref, refs[:count], weight_ref, sems
    )


def late_body(facts_ref, own_ref, other_ref, early_ref, *refs):
    count = len(LATE) * PIECES
    own_out_ref, other_out_ref, weight_ref, sems = refs[count:]
    total = group_contexts(LATE, facts_ref, own_ref, other_ref, refs[:count], weight_ref, sems)
    total = by_z(total + early_ref[...])
    for tile in range(4):
        target = (own_out_ref, other_out_ref)[tile // 2]
        target[tile % 2] = total[:, tile * PATCH : (tile + 1) * PATCH].astype(jnp.bfloat16)


def encode(body, groups, out_shape, facts, arrays, pieces):
    in_vmem = pl.BlockSpec(memory_space=pltpu.VMEM)
    taken = [pieces[group * PIECES + k] for group in groups for k in range(PIECES)]
    if groups == EARLY:
        taken = [pltpu.with_memory_space_constraint(t, pltpu.HBM) for t in taken]
    flops = 2 * 4 * PATCH * D * 4 * WIDTH * len(groups)
    return pl.pallas_call(
        body,
        out_shape=out_shape,
        in_specs=[pl.BlockSpec(memory_space=pltpu.SMEM)]
        + [in_vmem] * len(arrays)
        + [pl.BlockSpec(memory_space=pl.ANY)] * len(taken),
        out_specs=jax.tree.map(lambda _: in_vmem, out_shape),
        scratch_shapes=[
            pltpu.VMEM((len(groups), 2, 2, D // 4, 4 * WIDTH), jnp.bfloat16),
            pltpu.SemaphoreType.DMA((len(groups), PIECES)),
        ],
        compiler_params=vmem_params(),
        cost_estimate=pl.CostEstimate(
            flops=flops, bytes_accessed=len(groups) * D * 8 * WIDTH, transcendentals=0
        ),
        name=body.__name__,
    )(facts, *arrays, *taken)


def around_y(block):
    length = 2 * GROUPS
    half = block.shape[0] // 2

    def ways(sign):
        pairs = []
        for y in range(length):
            for core in range(2):
                to = (y + (sign if core == 0 else -sign)) % length
                pairs.append(tuple(p // 4 * 8 + core * 4 + p % 4 for p in (y, to)))
        return pairs

    halves = [block[:half], block[half:]]
    rising, falling = list(halves), list(halves)
    found = {(0, 0): halves[0], (0, 1): halves[1]}
    for hop in range(1, length // 2 + 1):
        last = 2 * hop == length
        for k in range(2):
            if not last or k == 0:
                rising[k] = lax.ppermute(rising[k], ("y_hi", "core", "tensor"), ways(1))
                found[length - hop, k] = rising[k]
            if not last or k == 1:
                falling[k] = lax.ppermute(falling[k], ("y_hi", "core", "tensor"), ways(-1))
                found[hop, k] = falling[k]
    return [
        found[group + k // 2 * GROUPS, k % 2] for group in range(GROUPS) for k in range(PIECES)
    ]


def local(tiles, tile_counts, doc_order, qkv_weight, out_weight):
    bal_hi, bal_lo = lax.axis_index("bal_hi"), lax.axis_index("bal_lo")
    tensor = lax.axis_index("tensor")
    swap = [(0, 1), (1, 0)]

    place = bal_lo * 8 + bal_hi * 4 + tensor
    y = lax.axis_index("y_hi") * 4 + tensor
    core = lax.axis_index("core")
    here = jnp.stack([bal_hi * 2 + bal_lo, place, y, core]).astype(jnp.int32)
    facts = jnp.concatenate([here, tile_counts[0], doc_order[0]])

    outbound = rotate(facts, tiles[0, 0])
    outbound, qkv_weight, out_weight = lax.optimization_barrier((outbound, qkv_weight, out_weight))
    arrived = lax.all_to_all(outbound, ("bal_lo", "bal_hi", "tensor"), 0, 0, tiled=True)

    keep, send = cut(facts, qkv_weight, out_weight)
    got = lax.ppermute(send, "core", swap)
    first, second = jnp.where(core == 0, keep, got), jnp.where(core == 0, got, keep)
    both = jnp.concatenate([first, second])
    block = lax.all_gather(both, "z", axis=0, tiled=True)
    pieces = around_y(block)
    source, normed = normalise(facts, arrived.reshape(4, D, PATCH))
    other = lax.ppermute(normed, "core", swap)

    early = jax.ShapeDtypeStruct((D, 4 * PATCH), jnp.float32)
    part = jax.ShapeDtypeStruct((2, D, PATCH), jnp.bfloat16)
    total = encode(early_body, EARLY, early, facts, (normed, other), pieces)
    own_part, other_part = encode(
        late_body, LATE, (part, part), facts, (normed, other, total), pieces
    )
    back_part = lax.ppermute(other_part, "core", swap)
    encoded = (
        source.astype(jnp.float32) + own_part.astype(jnp.float32) + back_part.astype(jnp.float32)
    ).astype(jnp.bfloat16)
    returned = lax.all_to_all(
        encoded.reshape(8, D // 4, PATCH), ("bal_hi", "tensor"), 0, 0, tiled=True
    )
    return returned[None]


def solution(mesh):
    z = mesh.shape["dp"] // 4
    devices = mesh.devices.reshape(z, 2, 2, 2, 2, 4)
    fine = Mesh(devices, ("z", "y_hi", "core", "bal_hi", "bal_lo", "tensor"))
    dp, bal = ("z", "y_hi", "core"), ("bal_hi", "bal_lo")
    placed = (
        P(dp, bal, None, "tensor", None),
        P(dp, None),
        P(dp, None),
        P(None, dp, "tensor"),
        P(dp, "tensor"),
    )
    return jax.shard_map(
        local, mesh=fine, in_specs=placed, out_specs=P(dp, bal, "tensor", None), check_vma=False
    )
```

```python
import jax
import jax.numpy as jnp
from jax import lax
from jax.experimental import pallas as pl
from jax.experimental.pallas import tpu as pltpu
from jax.sharding import Mesh, PartitionSpec as P

D = 1280
HDIM = 80
PATCH = 128
SLOTS = 16
DOCS = 4
BAL, PLACE, RING, CORE, COUNTS, ORDER = 0, 1, 2, 3, 4, 4 + DOCS
ZS = 16
GROUPS = 4
PIECES = 4
ORDERED = (2, 1, 3, 0)
LOCAL = 2
WIDTH = LOCAL * HDIM
EPSILON = 1e-06
VMEM = 32 * 2**20
LOG2E = 1.4426950408889634


def vmem_params():
    return pltpu.CompilerParams(vmem_limit_bytes=VMEM)


def cut_body(facts_ref, qkv_ref, out_ref, keep_ref, send_ref):
    halves = []
    for core in range(2):
        low = core * WIDTH
        kinds = [qkv_ref[k, :, low : low + WIDTH] for k in range(3)] + [out_ref[:, low : low + WIDTH]]
        halves.append(jnp.concatenate(kinds, axis=1))

    def put(keep, send):
        keep_ref[...] = halves[keep]
        send_ref[...] = halves[send]

    pl.when(facts_ref[CORE] == 0)(lambda: put(0, 1))
    pl.when(facts_ref[CORE] != 0)(lambda: put(1, 0))


def cut(facts, qkv_weight, out_weight):
    in_vmem = pl.BlockSpec(memory_space=pltpu.VMEM)
    half = jax.ShapeDtypeStruct((out_weight.shape[0], 4 * WIDTH), jnp.bfloat16)
    return pl.pallas_call(
        cut_body,
        out_shape=(half, half),
        in_specs=[pl.BlockSpec(memory_space=pltpu.SMEM), in_vmem, in_vmem],
        out_specs=(in_vmem, in_vmem),
        compiler_params=vmem_params(),
        name="cut",
    )(facts, *[pltpu.with_memory_space_constraint(w, pltpu.HBM) for w in (qkv_weight, out_weight)])


def in_turn(facts_ref):
    first, turns = 0, []
    for turn in range(DOCS):
        doc = facts_ref[ORDER + turn]
        count = facts_ref[COUNTS + doc]
        turns.append((doc, first, count))
        first = first + count
    return turns


def rotate_body(facts_ref, tiles_ref, out_ref, held_ref, in_sems, out_sems):
    start = 0
    for doc, first, _ in in_turn(facts_ref):
        start = jnp.where(doc == facts_ref[BAL], first, start)
    arriving = [
        pltpu.make_async_copy(tiles_ref.at[slot], held_ref.at[slot], in_sems.at[slot])
        for slot in range(SLOTS)
    ]
    leaving = [
        pltpu.make_async_copy(
            held_ref.at[slot], out_ref.at[(slot + start) & (SLOTS - 1)], out_sems.at[slot]
        )
        for slot in range(SLOTS)
    ]
    for copy in arriving:
        copy.start()
    for slot in range(SLOTS):
        arriving[slot].wait()
        leaving[slot].start()
    for copy in leaving:
        copy.wait()


def rotate(facts, tiles):
    return pl.pallas_call(
        rotate_body,
        out_shape=jax.ShapeDtypeStruct(tiles.shape, tiles.dtype),
        in_specs=[pl.BlockSpec(memory_space=pltpu.SMEM), pl.BlockSpec(memory_space=pl.ANY)],
        out_specs=pl.BlockSpec(memory_space=pl.ANY),
        scratch_shapes=[
            pltpu.VMEM(tiles.shape, tiles.dtype),
            pltpu.SemaphoreType.DMA((SLOTS,)),
            pltpu.SemaphoreType.DMA((SLOTS,)),
        ],
        compiler_params=vmem_params(),
        name="rotate",
    )(facts, pltpu.with_memory_space_constraint(tiles, pltpu.HBM))


def by_half(rows):
    parts = rows.reshape(ZS, 2, D // (2 * ZS), rows.shape[-1])
    return jnp.concatenate([parts[:, h].reshape(D // 2, rows.shape[-1]) for h in range(2)], axis=0)


def by_z(rows):
    parts = rows.reshape(2, ZS, 1, D // (2 * ZS), rows.shape[-1])
    return jnp.concatenate([parts[0], parts[1]], axis=1).reshape(D, rows.shape[-1])


def normalise_body(facts_ref, tile_ref, source_ref, normed_ref):
    tile = tile_ref[0]
    source_ref[0] = tile
    values = tile.astype(jnp.float32)
    center = values - jnp.mean(values, axis=0, keepdims=True)
    spread = jnp.mean(center * center, axis=0, keepdims=True)
    normed = by_half(center * lax.rsqrt(spread + EPSILON))
    normed_ref[0] = normed.T.astype(jnp.bfloat16)


def normalise(facts, arrived):
    def pick(j, facts_ref):
        packed = facts_ref[PLACE] + j * SLOTS
        owner = 0
        for doc, first, count in in_turn(facts_ref):
            owner = jnp.where((first <= packed) & (packed < first + count), doc, owner)
        return (owner & 1) * 2 + (owner >> 1), 0, 0

    def same(j, *_):
        return j, 0, 0

    return pl.pallas_call(
        normalise_body,
        out_shape=(
            jax.ShapeDtypeStruct((2, D, PATCH), jnp.bfloat16),
            jax.ShapeDtypeStruct((2, PATCH, D), jnp.bfloat16),
        ),
        grid_spec=pltpu.PrefetchScalarGridSpec(
            num_scalar_prefetch=1,
            grid=(2,),
            in_specs=[pl.BlockSpec((1, D, PATCH), pick)],
            out_specs=(pl.BlockSpec((1, D, PATCH), same), pl.BlockSpec((1, PATCH, D), same)),
        ),
        compiler_params=vmem_params(),
        name="normalise",
    )(facts, arrived)


def attend(qkv):
    pairs = [(tile, head) for tile in range(4) for head in range(LOCAL)]

    def part(kind, tile, head):
        low = kind * WIDTH + head * HDIM
        return qkv[low : low + HDIM, tile * PATCH : (tile + 1) * PATCH]

    scores = [
        lax.dot_general(
            part(1, *pair), part(0, *pair), (((0,), (0,)), ((), ())),
            preferred_element_type=jnp.float32,
        )
        for pair in pairs
    ]
    scale = HDIM ** (-0.5) * LOG2E
    powers = [jnp.exp2((s - jnp.max(s, axis=0, keepdims=True)) * scale) for s in scores]
    inverse = [1.0 / jnp.sum(p, axis=0, keepdims=True) for p in powers]
    contexts = [
        (
            jnp.dot(part(2, *pair), p.astype(jnp.bfloat16), preferred_element_type=jnp.float32) * i
        ).astype(jnp.bfloat16)
        for pair, p, i in zip(pairs, powers, inverse)
    ]
    return jnp.concatenate(
        [
            jnp.concatenate(contexts[tile * LOCAL : (tile + 1) * LOCAL], axis=0)
            for tile in range(4)
        ],
        axis=1,
    )


def group_contexts(groups, facts_ref, own_ref, other_ref, pieces, weight_ref, sems):
    def copies(n, group):
        made = []
        for k in range(PIECES):
            away = (1 - 2 * facts_ref[CORE]) * (group + k // 2 * GROUPS)
            y_hi = ((facts_ref[RING] + away) >> 2) & 1
            made.append(
                pltpu.make_async_copy(
                    pieces[n * PIECES + k], weight_ref.at[n, y_hi, k % 2], sems.at[n, k]
                )
            )
        return made

    for n, group in enumerate(groups):
        for copy in copies(n, group):
            copy.start()
    normed = jnp.concatenate(
        [ref[...].reshape(2 * PATCH, D) for ref in (own_ref, other_ref)], axis=0
    )
    contexts, outs = [], []
    for n, group in enumerate(groups):
        for copy in copies(n, group):
            copy.wait()
        weight = weight_ref[n].reshape(D, 4 * WIDTH)
        projected = jnp.dot(normed, weight[:, : 3 * WIDTH], preferred_element_type=jnp.float32)
        contexts.append(attend(projected.astype(jnp.bfloat16).T))
        outs.append(weight[:, 3 * WIDTH :])
    return jnp.dot(
        jnp.concatenate(outs, axis=1),
        jnp.concatenate(contexts, axis=0),
        preferred_element_type=jnp.float32,
    )


def encode_body(facts_ref, own_ref, other_ref, *refs):
    outs, (weight_ref, sems) = refs[-4:-2], refs[-2:]
    total = group_contexts(ORDERED, facts_ref, own_ref, other_ref, refs[:-4], weight_ref, sems)
    total = by_z(total)
    for tile in range(4):
        block = total[:, tile * PATCH : (tile + 1) * PATCH]
        outs[tile // 2][tile % 2] = block.astype(jnp.bfloat16)


def encode(facts, own, other, pieces):
    in_vmem = pl.BlockSpec(memory_space=pltpu.VMEM)
    part = jax.ShapeDtypeStruct((2, D, PATCH), jnp.bfloat16)
    taken = [pieces[group * PIECES + k] for group in ORDERED for k in range(PIECES)]
    settled = len(taken) - 2
    taken = [
        pltpu.with_memory_space_constraint(t, pltpu.HBM) if i < settled else t
        for i, t in enumerate(taken)
    ]
    return pl.pallas_call(
        encode_body,
        out_shape=(part, part),
        in_specs=[pl.BlockSpec(memory_space=pltpu.SMEM), in_vmem, in_vmem]
        + [pl.BlockSpec(memory_space=pl.ANY)] * len(taken),
        out_specs=(in_vmem, in_vmem),
        scratch_shapes=[
            pltpu.VMEM((GROUPS, 2, 2, D // 4, 4 * WIDTH), jnp.bfloat16),
            pltpu.SemaphoreType.DMA((GROUPS, PIECES)),
        ],
        compiler_params=vmem_params(),
        name="encode",
    )(facts, own, other, *taken)


def around_y(block):
    length = 2 * GROUPS
    half = block.shape[0] // 2

    def ways(sign):
        pairs = []
        for y in range(length):
            for core in range(2):
                to = (y + (sign if core == 0 else -sign)) % length
                pairs.append(tuple(p // 4 * 8 + core * 4 + p % 4 for p in (y, to)))
        return pairs

    halves = [block[:half], block[half:]]
    rising, falling = list(halves), list(halves)
    found = {(0, 0): halves[0], (0, 1): halves[1]}
    for hop in range(1, length // 2 + 1):
        last = 2 * hop == length
        for k in range(2):
            if not last or k == 0:
                rising[k] = lax.ppermute(rising[k], ("y_hi", "core", "tensor"), ways(1))
                found[length - hop, k] = rising[k]
            if not last or k == 1:
                falling[k] = lax.ppermute(falling[k], ("y_hi", "core", "tensor"), ways(-1))
                found[hop, k] = falling[k]
    return [
        found[group + k // 2 * GROUPS, k % 2] for group in range(GROUPS) for k in range(PIECES)
    ]


def local(tiles, tile_counts, doc_order, qkv_weight, out_weight):
    bal_hi, bal_lo = lax.axis_index("bal_hi"), lax.axis_index("bal_lo")
    tensor = lax.axis_index("tensor")
    swap = [(0, 1), (1, 0)]

    place = bal_lo * 8 + bal_hi * 4 + tensor
    y = lax.axis_index("y_hi") * 4 + tensor
    core = lax.axis_index("core")
    here = jnp.stack([bal_hi * 2 + bal_lo, place, y, core]).astype(jnp.int32)
    facts = jnp.concatenate([here, tile_counts[0], doc_order[0]])

    outbound = rotate(facts, tiles[0, 0])
    outbound, qkv_weight, out_weight = lax.optimization_barrier((outbound, qkv_weight, out_weight))
    arrived = lax.all_to_all(outbound, ("bal_lo", "bal_hi", "tensor"), 0, 0, tiled=True)

    keep, send = cut(facts, qkv_weight, out_weight)
    got = lax.ppermute(send, "core", swap)
    first, second = jnp.where(core == 0, keep, got), jnp.where(core == 0, got, keep)
    both = jnp.concatenate([first, second])
    block = lax.all_gather(both, "z", axis=0, tiled=True)
    pieces = around_y(block)
    source, normed = normalise(facts, arrived.reshape(4, D, PATCH))
    other = lax.ppermute(normed, "core", swap)

    own_part, other_part = encode(facts, normed, other, pieces)
    back_part = lax.ppermute(other_part, "core", swap)
    encoded = (
        source.astype(jnp.float32) + own_part.astype(jnp.float32) + back_part.astype(jnp.float32)
    ).astype(jnp.bfloat16)
    returned = lax.all_to_all(
        encoded.reshape(8, D // 4, PATCH), ("bal_hi", "tensor"), 0, 0, tiled=True
    )
    return returned[None]


def solution(mesh):
    z = mesh.shape["dp"] // 4
    devices = mesh.devices.reshape(z, 2, 2, 2, 2, 4)
    fine = Mesh(devices, ("z", "y_hi", "core", "bal_hi", "bal_lo", "tensor"))
    dp, bal = ("z", "y_hi", "core"), ("bal_hi", "bal_lo")
    placed = (
        P(dp, bal, None, "tensor", None),
        P(dp, None),
        P(dp, None),
        P(None, dp, "tensor"),
        P(dp, "tensor"),
    )
    return jax.shard_map(
        local, mesh=fine, in_specs=placed, out_specs=P(dp, bal, "tensor", None), check_vma=False
    )
```

```python
import jax
import jax.numpy as jnp
from jax import lax
from jax.experimental import pallas as pl
from jax.experimental.pallas import tpu as pltpu
from jax.sharding import Mesh, PartitionSpec as P

D = 1280
HDIM = 80
PATCH = 128
SLOTS = 16
DOCS = 4
BAL, PLACE, RING, CORE, COUNTS, ORDER = 0, 1, 2, 3, 4, 4 + DOCS
ZS = 16
GROUPS = 4
PIECES = 4
EARLY, LATE = (2, 1, 3), (0,)
LOCAL = 2
WIDTH = LOCAL * HDIM
EPSILON = 1e-06
VMEM = 32 * 2**20
LOG2E = 1.4426950408889634


def vmem_params():
    return pltpu.CompilerParams(vmem_limit_bytes=VMEM)


def cut_body(facts_ref, qkv_ref, out_ref, keep_ref, send_ref):
    halves = []
    for core in range(2):
        low = core * WIDTH
        kinds = [qkv_ref[k, :, low : low + WIDTH] for k in range(3)] + [out_ref[:, low : low + WIDTH]]
        halves.append(jnp.concatenate(kinds, axis=1))

    def put(keep, send):
        keep_ref[...] = halves[keep]
        send_ref[...] = halves[send]

    pl.when(facts_ref[CORE] == 0)(lambda: put(0, 1))
    pl.when(facts_ref[CORE] != 0)(lambda: put(1, 0))


def cut(facts, qkv_weight, out_weight):
    in_vmem = pl.BlockSpec(memory_space=pltpu.VMEM)
    half = jax.ShapeDtypeStruct((out_weight.shape[0], 4 * WIDTH), jnp.bfloat16)
    return pl.pallas_call(
        cut_body,
        out_shape=(half, half),
        in_specs=[pl.BlockSpec(memory_space=pltpu.SMEM), in_vmem, in_vmem],
        out_specs=(in_vmem, in_vmem),
        compiler_params=vmem_params(),
        name="cut",
    )(facts, *[pltpu.with_memory_space_constraint(w, pltpu.HBM) for w in (qkv_weight, out_weight)])


def in_turn(facts_ref):
    first, turns = 0, []
    for turn in range(DOCS):
        doc = facts_ref[ORDER + turn]
        count = facts_ref[COUNTS + doc]
        turns.append((doc, first, count))
        first = first + count
    return turns


def rotate_body(facts_ref, tiles_ref, out_ref, held_ref, in_sems, out_sems):
    start = 0
    for doc, first, _ in in_turn(facts_ref):
        start = jnp.where(doc == facts_ref[BAL], first, start)
    arriving = [
        pltpu.make_async_copy(tiles_ref.at[slot], held_ref.at[slot], in_sems.at[slot])
        for slot in range(SLOTS)
    ]
    leaving = [
        pltpu.make_async_copy(
            held_ref.at[slot], out_ref.at[(slot + start) & (SLOTS - 1)], out_sems.at[slot]
        )
        for slot in range(SLOTS)
    ]
    for copy in arriving:
        copy.start()
    for slot in range(SLOTS):
        arriving[slot].wait()
        leaving[slot].start()
    for copy in leaving:
        copy.wait()


def rotate(facts, tiles):
    return pl.pallas_call(
        rotate_body,
        out_shape=jax.ShapeDtypeStruct(tiles.shape, tiles.dtype),
        in_specs=[pl.BlockSpec(memory_space=pltpu.SMEM), pl.BlockSpec(memory_space=pl.ANY)],
        out_specs=pl.BlockSpec(memory_space=pl.ANY),
        scratch_shapes=[
            pltpu.VMEM(tiles.shape, tiles.dtype),
            pltpu.SemaphoreType.DMA((SLOTS,)),
            pltpu.SemaphoreType.DMA((SLOTS,)),
        ],
        compiler_params=vmem_params(),
        name="rotate",
    )(facts, pltpu.with_memory_space_constraint(tiles, pltpu.HBM))


def by_half(rows):
    parts = rows.reshape(ZS, 2, D // (2 * ZS), rows.shape[-1])
    return jnp.concatenate([parts[:, h].reshape(D // 2, rows.shape[-1]) for h in range(2)], axis=0)


def by_z(rows):
    parts = rows.reshape(2, ZS, 1, D // (2 * ZS), rows.shape[-1])
    return jnp.concatenate([parts[0], parts[1]], axis=1).reshape(D, rows.shape[-1])


def normalise_body(facts_ref, tile_ref, source_ref, normed_ref):
    tile = tile_ref[0]
    source_ref[0] = tile
    values = tile.astype(jnp.float32)
    center = values - jnp.mean(values, axis=0, keepdims=True)
    spread = jnp.mean(center * center, axis=0, keepdims=True)
    normed = by_half(center * lax.rsqrt(spread + EPSILON))
    normed_ref[0] = normed.T.astype(jnp.bfloat16)


def normalise(facts, arrived):
    def pick(j, facts_ref):
        packed = facts_ref[PLACE] + j * SLOTS
        owner = 0
        for doc, first, count in in_turn(facts_ref):
            owner = jnp.where((first <= packed) & (packed < first + count), doc, owner)
        return (owner & 1) * 2 + (owner >> 1), 0, 0

    def same(j, *_):
        return j, 0, 0

    return pl.pallas_call(
        normalise_body,
        out_shape=(
            jax.ShapeDtypeStruct((2, D, PATCH), jnp.bfloat16),
            jax.ShapeDtypeStruct((2, PATCH, D), jnp.bfloat16),
        ),
        grid_spec=pltpu.PrefetchScalarGridSpec(
            num_scalar_prefetch=1,
            grid=(2,),
            in_specs=[pl.BlockSpec((1, D, PATCH), pick)],
            out_specs=(pl.BlockSpec((1, D, PATCH), same), pl.BlockSpec((1, PATCH, D), same)),
        ),
        compiler_params=vmem_params(),
        name="normalise",
    )(facts, arrived)


def attend(qkv):
    count = qkv.shape[1] // PATCH
    pairs = [(tile, head) for tile in range(count) for head in range(LOCAL)]

    def part(kind, tile, head):
        low = kind * WIDTH + head * HDIM
        return qkv[low : low + HDIM, tile * PATCH : (tile + 1) * PATCH]

    scores = [
        lax.dot_general(
            part(1, *pair), part(0, *pair), (((0,), (0,)), ((), ())),
            preferred_element_type=jnp.float32,
        )
        for pair in pairs
    ]
    scale = HDIM ** (-0.5) * LOG2E
    powers = [jnp.exp2((s - jnp.max(s, axis=0, keepdims=True)) * scale) for s in scores]
    inverse = [1.0 / jnp.sum(p, axis=0, keepdims=True) for p in powers]
    contexts = [
        (
            jnp.dot(part(2, *pair), p.astype(jnp.bfloat16), preferred_element_type=jnp.float32) * i
        ).astype(jnp.bfloat16)
        for pair, p, i in zip(pairs, powers, inverse)
    ]
    return jnp.concatenate(
        [
            jnp.concatenate(contexts[tile * LOCAL : (tile + 1) * LOCAL], axis=0)
            for tile in range(count)
        ],
        axis=1,
    )


def group_contexts(groups, facts_ref, normed_refs, pieces, weight_ref, sems):
    def copies(n, group):
        made = []
        for k in range(PIECES):
            away = (1 - 2 * facts_ref[CORE]) * (group + k // 2 * GROUPS)
            y_hi = ((facts_ref[RING] + away) >> 2) & 1
            made.append(
                pltpu.make_async_copy(
                    pieces[n * PIECES + k], weight_ref.at[n, y_hi, k % 2], sems.at[n, k]
                )
            )
        return made

    for n, group in enumerate(groups):
        for copy in copies(n, group):
            copy.start()
    normed = jnp.concatenate(
        [ref[...].reshape(2 * PATCH, D) for ref in normed_refs], axis=0
    )
    contexts, outs = [], []
    for n, group in enumerate(groups):
        for copy in copies(n, group):
            copy.wait()
        weight = weight_ref[n].reshape(D, 4 * WIDTH)
        projected = jnp.dot(normed, weight[:, : 3 * WIDTH], preferred_element_type=jnp.float32)
        contexts.append(attend(projected.astype(jnp.bfloat16).T))
        outs.append(weight[:, 3 * WIDTH :])
    return jnp.dot(
        jnp.concatenate(outs, axis=1),
        jnp.concatenate(contexts, axis=0),
        preferred_element_type=jnp.float32,
    )


def early_body(facts_ref, own_ref, other_ref, *refs):
    own_total_ref, other_total_ref, weight_ref, sems = refs[-4:]
    total = group_contexts(EARLY, facts_ref, (own_ref, other_ref), refs[:-4], weight_ref, sems)
    own_total_ref[...] = total[:, : 2 * PATCH]
    other_total_ref[...] = total[:, 2 * PATCH :]


def late_body(facts_ref, normed_ref, early_ref, *refs):
    out_ref, weight_ref, sems = refs[-3:]
    total = group_contexts(LATE, facts_ref, (normed_ref,), refs[:-3], weight_ref, sems)
    total = by_z(total + early_ref[...])
    for tile in range(2):
        out_ref[tile] = total[:, tile * PATCH : (tile + 1) * PATCH].astype(jnp.bfloat16)


def encode(body, groups, out_shape, facts, arrays, pieces):
    in_vmem = pl.BlockSpec(memory_space=pltpu.VMEM)
    taken = [pieces[group * PIECES + k] for group in groups for k in range(PIECES)]
    if groups == EARLY:
        taken = [pltpu.with_memory_space_constraint(t, pltpu.HBM) for t in taken]
    flops = 2 * 4 * PATCH * D * 4 * WIDTH * len(groups)
    return pl.pallas_call(
        body,
        out_shape=out_shape,
        in_specs=[pl.BlockSpec(memory_space=pltpu.SMEM)]
        + [in_vmem] * len(arrays)
        + [pl.BlockSpec(memory_space=pl.ANY)] * len(taken),
        out_specs=jax.tree.map(lambda _: in_vmem, out_shape),
        scratch_shapes=[
            pltpu.VMEM((len(groups), 2, 2, D // 4, 4 * WIDTH), jnp.bfloat16),
            pltpu.SemaphoreType.DMA((len(groups), PIECES)),
        ],
        compiler_params=vmem_params(),
        cost_estimate=pl.CostEstimate(
            flops=flops, bytes_accessed=len(groups) * D * 8 * WIDTH, transcendentals=0
        ),
        name=body.__name__,
    )(facts, *arrays, *taken)


def around_y(block):
    length = 2 * GROUPS
    half = block.shape[0] // 2

    def ways(sign):
        pairs = []
        for y in range(length):
            for core in range(2):
                to = (y + (sign if core == 0 else -sign)) % length
                pairs.append(tuple(p // 4 * 8 + core * 4 + p % 4 for p in (y, to)))
        return pairs

    halves = [block[:half], block[half:]]
    rising, falling = list(halves), list(halves)
    found = {(0, 0): halves[0], (0, 1): halves[1]}
    for hop in range(1, length // 2 + 1):
        last = 2 * hop == length
        for k in range(2):
            if not last or k == 0:
                rising[k] = lax.ppermute(rising[k], ("y_hi", "core", "tensor"), ways(1))
                found[length - hop, k] = rising[k]
            if not last or k == 1:
                falling[k] = lax.ppermute(falling[k], ("y_hi", "core", "tensor"), ways(-1))
                found[hop, k] = falling[k]
    return [
        found[group + k // 2 * GROUPS, k % 2] for group in range(GROUPS) for k in range(PIECES)
    ]


def local(tiles, tile_counts, doc_order, qkv_weight, out_weight):
    bal_hi, bal_lo = lax.axis_index("bal_hi"), lax.axis_index("bal_lo")
    tensor = lax.axis_index("tensor")
    swap = [(0, 1), (1, 0)]

    place = bal_lo * 8 + bal_hi * 4 + tensor
    y = lax.axis_index("y_hi") * 4 + tensor
    core = lax.axis_index("core")
    here = jnp.stack([bal_hi * 2 + bal_lo, place, y, core]).astype(jnp.int32)
    facts = jnp.concatenate([here, tile_counts[0], doc_order[0]])

    outbound = rotate(facts, tiles[0, 0])
    outbound, qkv_weight, out_weight = lax.optimization_barrier((outbound, qkv_weight, out_weight))
    arrived = lax.all_to_all(outbound, ("bal_lo", "bal_hi", "tensor"), 0, 0, tiled=True)

    keep, send = cut(facts, qkv_weight, out_weight)
    got = lax.ppermute(send, "core", swap)
    first, second = jnp.where(core == 0, keep, got), jnp.where(core == 0, got, keep)
    both = jnp.concatenate([first, second])
    block = lax.all_gather(both, "z", axis=0, tiled=True)
    pieces = around_y(block)
    source, normed = normalise(facts, arrived.reshape(4, D, PATCH))
    other = lax.ppermute(normed, "core", swap)

    early = jax.ShapeDtypeStruct((D, 2 * PATCH), jnp.float32)
    part = jax.ShapeDtypeStruct((2, D, PATCH), jnp.bfloat16)
    own_total, other_total = encode(
        early_body, EARLY, (early, early), facts, (normed, other), pieces
    )
    other_part = encode(late_body, LATE, part, facts, (other, other_total), pieces)
    back_part = lax.ppermute(other_part, "core", swap)
    own_part = encode(late_body, LATE, part, facts, (normed, own_total), pieces)
    encoded = (
        source.astype(jnp.float32) + own_part.astype(jnp.float32) + back_part.astype(jnp.float32)
    ).astype(jnp.bfloat16)
    returned = lax.all_to_all(
        encoded.reshape(8, D // 4, PATCH), ("bal_hi", "tensor"), 0, 0, tiled=True
    )
    return returned[None]


def solution(mesh):
    z = mesh.shape["dp"] // 4
    devices = mesh.devices.reshape(z, 2, 2, 2, 2, 4)
    fine = Mesh(devices, ("z", "y_hi", "core", "bal_hi", "bal_lo", "tensor"))
    dp, bal = ("z", "y_hi", "core"), ("bal_hi", "bal_lo")
    placed = (
        P(dp, bal, None, "tensor", None),
        P(dp, None),
        P(dp, None),
        P(None, dp, "tensor"),
        P(dp, "tensor"),
    )
    return jax.shard_map(
        local, mesh=fine, in_specs=placed, out_specs=P(dp, bal, "tensor", None), check_vma=False
    )
```
